32 devices in a mesh: seq: 4 (over x, core), res: 8 (over z, y).
Axes of the slice: x: 2, y: 2, z: 4, core: 2. Of those that a mesh axis runs over, the one named last changes fastest.
Arguments:
- homolog_embedding: bfloat16 [16, 512, 256], P('seq', 'res'), may hold values from -6 to 6
- pair_input_rows: bfloat16 [512, 512, 128], P('res', 'seq'), may hold values from -256 to 256
- incoming_slope: bfloat16 [16, 512, 256], P('seq', 'res'), may hold values from -6 to 6
- rescale_factor: float32 [256], replicated, may hold values from 0.25 to 1.75
- probe_weights: bfloat16 [256, 256], replicated, may hold values from -0.375 to 0.375
- lookup_weights: bfloat16 [256, 256], replicated, may hold values from -0.375 to 0.375
- content_weights: bfloat16 [256, 256], replicated, may hold values from -0.375 to 0.375
- sigmoid_weights: bfloat16 [256, 256], replicated, may hold values from -0.375 to 0.375
- final_projection: bfloat16 [256, 256], replicated, may hold values from -0.375 to 0.375
- pair_bias_matrix: bfloat16 [128, 8], replicated, may hold values from -1 to 1
Outputs:
- alignment_rows_gradient: bfloat16 [16, 512, 256], P('seq', 'res')
- pair_input_gradient: bfloat16 [512, 512, 128], P('res', 'seq')
- layer_gain_gradient: float32 [256], replicated
- query_matrix_gradient: float32 [256, 256], replicated
- key_matrix_gradient: float32 [256, 256], replicated
- value_matrix_gradient: float32 [256, 256], replicated
- gate_matrix_gradient: float32 [256, 256], replicated
- final_projection_slope: float32 [256, 256], replicated
- pair_bias_matrix_gradient: float32 [128, 8], replicated
The draws below stay inside these ranges and needn't reach their ends.
All inputs are finite; a program needn't handle non-finite values.
Results may differ from the reference program's by a relative error of at most 0.0034.
The reference program's roundings to bfloat16 on the way count: a program that leaves them out, or rounds other values in their place, can miss the bound.
Values may be sent and summed in bfloat16 or wider, within the bound.
No kernel may reach another device: no remote copies, remote signals or barrier semaphores. Data moves between devices by JAX's collectives and lax.ppermute only.
A program may use at most 128 MiB of HBM per device.

```python
import functools
import math
import jax
import jax.numpy as jnp
from jax import lax

FEATURE_DEPTH = 256
H = 8
CZ = 128
HOMOLOG_NUMBER = 16
CHAIN_LENGTH = 512


def bias_weight_values(key):
    raw_values = jax.random.normal(jax.random.fold_in(key, 101), (CZ, H), jnp.float32) / math.sqrt(CZ)
    return jnp.clip(raw_values, -1.0, 1.0).astype(jnp.bfloat16).astype(jnp.float32)


def draw_pair_bias_matrix(key, part):
    return bias_weight_values(key).astype(jnp.bfloat16)


def draw_pair_input_rows(key, part):
    result = jnp.clip(jax.random.normal(jax.random.fold_in(key, 206), (CHAIN_LENGTH, CHAIN_LENGTH, CZ), jnp.float32), -6.0, 6.0)
    return jnp.clip(result, -256.0, 256.0).astype(jnp.bfloat16)


def shard_levels(own_key, dims, pieces, low, high):
    loudness = 1.0
    for position, parts in pieces:
        draws = jax.random.uniform(jax.random.fold_in(jax.random.fold_in(own_key, 6), position), (parts,), jnp.float32, low / len(pieces), high / len(pieces))
        loudness = loudness * jnp.repeat(jnp.exp(draws), dims[position] // parts).reshape((-1,) + (1,) * (len(dims) - 1 - position))
    return loudness


def centred(rng, dims, spread, reach, shards=(), held_as=jnp.bfloat16):
    gain = shard_levels(rng, dims, shards, -0.22, 0.18) if shards else 1.0
    entries = jax.random.normal(rng, dims, jnp.float32) * spread * gain
    return jnp.minimum(jnp.maximum(entries, -reach), reach).astype(held_as)


def setup_inputs(seed: int = 0) -> dict:
    streams_of = jax.random.split(jax.random.key(seed), 11)
    homolog_embedding = centred(streams_of[0], (HOMOLOG_NUMBER, CHAIN_LENGTH, FEATURE_DEPTH), 1.0, 6.0, ((0, 4), (1, 8)))
    pair_input_rows = draw_pair_input_rows(jax.random.fold_in(streams_of[10], 71), 0)
    incoming_slope = centred(streams_of[2], (HOMOLOG_NUMBER, CHAIN_LENGTH, FEATURE_DEPTH), 1.0, 6.0, ((0, 4), (1, 8)))
    rescale_factor = jnp.clip(1.0 + 0.15 * jax.random.normal(streams_of[3], (FEATURE_DEPTH,), jnp.float32), 0.25, 1.75)
    probe_weights = centred(streams_of[4], (FEATURE_DEPTH, FEATURE_DEPTH), FEATURE_DEPTH ** -0.5, 0.375)
    lookup_weights = centred(streams_of[5], (FEATURE_DEPTH, FEATURE_DEPTH), FEATURE_DEPTH ** -0.5, 0.375)
    content_weights = centred(streams_of[6], (FEATURE_DEPTH, FEATURE_DEPTH), FEATURE_DEPTH ** -0.5, 0.375)
    sigmoid_weights = centred(streams_of[7], (FEATURE_DEPTH, FEATURE_DEPTH), FEATURE_DEPTH ** -0.5, 0.375)
    final_projection = centred(streams_of[8], (FEATURE_DEPTH, FEATURE_DEPTH), FEATURE_DEPTH ** -0.5, 0.375)
    pair_bias_matrix = draw_pair_bias_matrix(jax.random.fold_in(streams_of[10], 71), 0)
    return dict(homolog_embedding=homolog_embedding, pair_input_rows=pair_input_rows, incoming_slope=incoming_slope, rescale_factor=rescale_factor, probe_weights=probe_weights, lookup_weights=lookup_weights, content_weights=content_weights, sigmoid_weights=sigmoid_weights, final_projection=final_projection, pair_bias_matrix=pair_bias_matrix)


def layer_norm_rows(alignment_block):
    content_vectors = alignment_block.astype(jnp.float32)
    centered = content_vectors - lax.optimization_barrier(jnp.mean(content_vectors, axis=-1, keepdims=True))
    inverse_deviation = lax.rsqrt(lax.optimization_barrier(jnp.mean(centered * centered, axis=-1, keepdims=True)) + 1e-05)
    return (centered * inverse_deviation, inverse_deviation)

def row_backward(bias_full, head_count, dbias_total, row_inputs):
    probe_vectors, keys_row, values_row, gate_row, derivative_modulated = row_inputs
    query_total, channel_width = probe_vectors.shape
    key_count = keys_row.shape[0]
    head_width = channel_width // head_count
    softmax_scale = 1.0 / math.sqrt(head_width)
    query_heads = probe_vectors.reshape(query_total, head_count, head_width).astype(jnp.float32)
    key_heads = keys_row.reshape(key_count, head_count, head_width).astype(jnp.float32)
    value_heads = values_row.reshape(key_count, head_count, head_width).astype(jnp.float32)
    scores = jnp.einsum('ihd,jhd->hij', query_heads, key_heads) * softmax_scale + bias_full.astype(jnp.float32)
    weights_soft = jax.nn.softmax(scores, axis=-1)
    weights_half = weights_soft.astype(jnp.bfloat16)
    attended = jnp.einsum('hij,jhd->ihd', weights_half.astype(jnp.float32), value_heads).reshape(query_total, channel_width)
    modulated_result = (gate_row * attended).astype(jnp.bfloat16)
    grad_attended = (derivative_modulated * gate_row).astype(jnp.bfloat16)
    derivative_logits_sigmoid = (derivative_modulated * attended * gate_row * (1.0 - gate_row)).astype(jnp.bfloat16)
    grad_heads = grad_attended.reshape(query_total, head_count, head_width).astype(jnp.float32)
    grad_weights = jnp.einsum('ihd,jhd->hij', grad_heads, value_heads)
    row_inner = lax.optimization_barrier(jnp.sum(weights_soft * grad_weights, axis=-1, keepdims=True))
    grad_scores = weights_soft * (grad_weights - row_inner)
    scores_half = grad_scores.astype(jnp.bfloat16).astype(jnp.float32)
    derivative_probe_weights = (jnp.einsum('hij,jhd->ihd', scores_half, key_heads) * softmax_scale).astype(jnp.bfloat16)
    derivative_lookup_weights = jnp.einsum('hij,ihd->jhd', scores_half, query_heads) * softmax_scale
    derivative_content_weights = jnp.einsum('hij,ihd->jhd', weights_half.astype(jnp.float32), grad_heads)
    outputs = (modulated_result, derivative_logits_sigmoid, derivative_probe_weights.reshape(query_total, channel_width), derivative_lookup_weights.reshape(key_count, channel_width), derivative_content_weights.reshape(key_count, channel_width))
    return (dbias_total + grad_scores, outputs)

def reference(homolog_embedding, pair_input_rows, incoming_slope, rescale_factor, probe_weights, lookup_weights, content_weights, sigmoid_weights, final_projection, pair_bias_matrix):
    highest = lax.Precision.HIGHEST
    standardized_rows, inverse_deviation = layer_norm_rows(homolog_embedding)
    rescaled_embedding = (standardized_rows * rescale_factor).astype(jnp.bfloat16)
    rescaled_plain = rescaled_embedding.reshape(-1, FEATURE_DEPTH)
    probe_vectors = jnp.dot(rescaled_plain, probe_weights, preferred_element_type=jnp.float32).astype(jnp.bfloat16).reshape(HOMOLOG_NUMBER, CHAIN_LENGTH, FEATURE_DEPTH)
    lookup_vectors = jnp.dot(rescaled_plain, lookup_weights, preferred_element_type=jnp.float32).astype(jnp.bfloat16).reshape(HOMOLOG_NUMBER, CHAIN_LENGTH, FEATURE_DEPTH)
    content_vectors = jnp.dot(rescaled_plain, content_weights, preferred_element_type=jnp.float32).astype(jnp.bfloat16).reshape(HOMOLOG_NUMBER, CHAIN_LENGTH, FEATURE_DEPTH)
    sigmoid_factors = jax.nn.sigmoid(jnp.dot(rescaled_plain, sigmoid_weights, preferred_element_type=jnp.float32)).reshape(HOMOLOG_NUMBER, CHAIN_LENGTH, FEATURE_DEPTH)
    incoming_slope_plain = incoming_slope.reshape(-1, FEATURE_DEPTH)
    derivative_modulated = jnp.dot(incoming_slope_plain, final_projection.T, preferred_element_type=jnp.float32).reshape(HOMOLOG_NUMBER, CHAIN_LENGTH, FEATURE_DEPTH)
    bias_flat = jnp.dot(pair_input_rows.reshape(-1, CZ), pair_bias_matrix, preferred_element_type=jnp.float32).astype(jnp.bfloat16)
    bias_full = jnp.transpose(bias_flat.reshape(CHAIN_LENGTH, CHAIN_LENGTH, H), (2, 0, 1))
    dbias_init = jnp.zeros((H, CHAIN_LENGTH, CHAIN_LENGTH), jnp.float32)
    dbias_total, row_results = lax.scan(functools.partial(row_backward, bias_full, H), dbias_init, (probe_vectors, lookup_vectors, content_vectors, sigmoid_factors, derivative_modulated))
    modulated_result, derivative_logits_sigmoid, derivative_probe_weights, derivative_lookup_weights, derivative_content_weights = row_results
    probe_plain = derivative_probe_weights.reshape(-1, FEATURE_DEPTH)
    sigmoid_factor_plain = derivative_logits_sigmoid.reshape(-1, FEATURE_DEPTH)
    lookup_plain = derivative_lookup_weights.reshape(-1, FEATURE_DEPTH)
    content_plain = derivative_content_weights.reshape(-1, FEATURE_DEPTH)
    final_projection_slope = jnp.dot(modulated_result.reshape(-1, FEATURE_DEPTH).T, incoming_slope_plain, preferred_element_type=jnp.float32)
    query_matrix_gradient = jnp.dot(rescaled_plain.T, probe_plain, preferred_element_type=jnp.float32)
    gate_matrix_gradient = jnp.dot(rescaled_plain.T, sigmoid_factor_plain, preferred_element_type=jnp.float32)
    normed_wide = rescaled_plain.astype(jnp.float32)
    key_matrix_gradient = jnp.dot(normed_wide.T, lookup_plain, precision=highest)
    value_matrix_gradient = jnp.dot(normed_wide.T, content_plain, precision=highest)
    derivative_rescaled = jnp.dot(probe_plain, probe_weights.T, preferred_element_type=jnp.float32) + jnp.dot(sigmoid_factor_plain, sigmoid_weights.T, preferred_element_type=jnp.float32) + jnp.dot(lookup_plain, lookup_weights.astype(jnp.float32).T, precision=highest) + jnp.dot(content_plain, content_weights.astype(jnp.float32).T, precision=highest)
    derivative_rescaled = derivative_rescaled.reshape(HOMOLOG_NUMBER, CHAIN_LENGTH, FEATURE_DEPTH)
    layer_gain_gradient = lax.optimization_barrier(jnp.sum(derivative_rescaled * standardized_rows, axis=(0, 1)))
    centered_scaled_gradient = derivative_rescaled * rescale_factor
    alignment_rows_gradient = (inverse_deviation * (centered_scaled_gradient - lax.optimization_barrier(jnp.mean(centered_scaled_gradient, axis=-1, keepdims=True)) - standardized_rows * lax.optimization_barrier(jnp.mean(centered_scaled_gradient * standardized_rows, axis=-1, keepdims=True)))).astype(jnp.bfloat16)
    dbias_half = dbias_total.astype(jnp.bfloat16)
    moved = jnp.transpose(dbias_half, (1, 2, 0))

    def project_row(bias_row):
        return jnp.dot(bias_row, pair_bias_matrix.T, preferred_element_type=jnp.float32).astype(jnp.bfloat16)
    pair_input_gradient = lax.map(project_row, moved)
    pair_bias_matrix_gradient = jnp.dot(pair_input_rows.reshape(-1, CZ).T, moved.reshape(-1, H), preferred_element_type=jnp.float32)
    return (alignment_rows_gradient, pair_input_gradient, layer_gain_gradient, query_matrix_gradient, key_matrix_gradient, value_matrix_gradient, gate_matrix_gradient, final_projection_slope, pair_bias_matrix_gradient)
```

```python
import functools
import math

import jax
import jax.numpy as jnp
from jax import lax
from jax.experimental import pallas as pl
from jax.experimental.pallas import tpu as pltpu
from jax.sharding import PartitionSpec as P

F32 = jnp.float32
BF16 = jnp.bfloat16


def exchange(value, axis, size, offset):
    return lax.ppermute(value, axis, [(i, i ^ offset) for i in range(size)])


def dot(a, b, dims=((1,), (0,))):
    return lax.dot_general(a, b, (dims, ((), ())), preferred_element_type=F32)


def norm_rows(block):
    wide = block.astype(F32)
    centered = wide - jnp.mean(wide, axis=-1, keepdims=True)
    inverse = lax.rsqrt(jnp.mean(centered * centered, axis=-1, keepdims=True) + 1e-05)
    return centered * inverse, inverse


def attention_kernel(
    n_res,
    n_seq,
    width,
    span,
    where,
    *refs,
):
    tokens = refs[:n_res]
    biases = refs[n_res : n_res + n_seq]
    head_w, out_w, gain_w = refs[n_res + n_seq : n_res + n_seq + 3]
    refs = refs[n_res + n_seq + 3 :]
    grads, (pair_keep, pair_send, sums_keep, sums_send) = refs[:n_res], refs[n_res : n_res + 4]
    hat_s, normed_s, slope_s, bias_s, dbias_s, grad_s, sums_s = refs[n_res + 4 :]
    row, last = pl.program_id(0), pl.num_programs(0) - 1
    r, s = where[0], where[1]
    own = tokens[0].shape[2]
    total = own * n_res
    part = total // n_seq
    channels = normed_s.shape[1]
    scale = 1.0 / math.sqrt(width)

    @pl.when(row == 0)
    def _():
        for m in range(n_seq):
            lane = pl.multiple_of(jnp.bitwise_xor(s, m) * part, part)
            for k in range(n_res):
                at = pl.multiple_of(jnp.bitwise_xor(r, k) * own, own)
                bias_s[pl.ds(at, own), pl.ds(lane, part)] = biases[m][k]
        dbias_s[...] = jnp.zeros_like(dbias_s)
        sums_s[...] = jnp.zeros_like(sums_s)

    for k in range(n_res):
        at = pl.multiple_of(jnp.bitwise_xor(r, k) * own, own)
        hat, _ = norm_rows(tokens[k][0, 0])
        hat_s[pl.ds(at, own), :] = hat
        normed_s[pl.ds(at, own), :] = (hat * gain_w[...]).astype(BF16)
        slope_s[pl.ds(at, own), :] = tokens[k][1, 0]

    normed = normed_s[...]
    slope = slope_s[...]
    weights = head_w[0]
    wq, wk, wv, wg = (weights[n * width : (n + 1) * width] for n in range(4))
    rows = ((1,), (1,))
    q = dot(normed, wq, rows).astype(BF16)
    k_ = dot(normed, wk, rows).astype(BF16)
    v = dot(normed, wv, rows).astype(BF16)
    gate = jax.nn.sigmoid(dot(normed, wg, rows))
    dgated = dot(slope, out_w[0], rows)
    datt = (dgated * gate).astype(BF16)
    q_t, k_t, v_t, datt_t = (jnp.transpose(x) for x in (q, k_, v, datt))

    gk_t = jnp.zeros((width, total), F32)
    gv_t = jnp.zeros((width, total), F32)
    gqs, atts = [], []
    for c in range(total // span):
        lo, hi = c * span, (c + 1) * span
        scores = dot(q[lo:hi], k_t) * scale + bias_s[lo:hi, :].astype(F32)
        top = jnp.max(scores, axis=-1, keepdims=True)
        e = jnp.exp(scores - top)
        soft = e * (1.0 / jnp.sum(e, axis=-1, keepdims=True))
        half = soft.astype(BF16)
        atts.append(dot(half, v))
        gv_t += dot(datt_t[:, lo:hi], half)
        dsoft = dot(datt[lo:hi], v_t)
        inner = jnp.sum(soft * dsoft, axis=-1, keepdims=True)
        dscores = soft * (dsoft - inner)
        dbias_s[lo:hi, :] += dscores
        dhalf = dscores.astype(BF16)
        gqs.append(dot(dhalf, k_) * scale)
        gk_t += dot(q_t[:, lo:hi], dhalf)
    att = jnp.concatenate(atts, axis=0)
    gated = (gate * att).astype(BF16)
    dgate = dgated * att * gate * (1.0 - gate)
    gq = jnp.concatenate(gqs, axis=0)
    grad_t = jnp.concatenate([jnp.transpose(gq), gk_t * scale, gv_t, jnp.transpose(dgate)], axis=0)
    grad_s[...] = jnp.transpose(grad_t)
    high_t = grad_t.astype(BF16)
    part_row = lax.broadcasted_iota(jnp.int32, grad_t.shape, 0)
    wide_rows = (part_row >= width) & (part_row < 3 * width)
    low_t = jnp.where(wide_rows, grad_t - high_t.astype(F32), 0.0).astype(BF16)
    sums_s[: 4 * width, :] += dot(high_t, normed) + dot(low_t, normed)
    sums_s[4 * width : 5 * width, :] += dot(jnp.transpose(gated), slope)
    grad_normed = dot(jnp.transpose(high_t), weights) + dot(jnp.transpose(low_t), weights)
    sums_s[5 * width : 5 * width + 1, :] += jnp.sum(grad_normed * hat_s[...], axis=0, keepdims=True)
    for k in range(n_res):
        at = pl.multiple_of(jnp.bitwise_xor(r, k) * own, own)
        grads[k][0] = grad_s[pl.ds(at, own), :].astype(BF16)

    @pl.when(row == last)
    def _():
        for m in range(n_seq):
            lane = pl.multiple_of(jnp.bitwise_xor(s, m) * part, part)
            (pair_send if m % 2 else pair_keep)[m // 2] = dbias_s[:, pl.ds(lane, part)]
        side = channels // 2
        core = jnp.bitwise_and(s, 1)
        sums_keep[...] = sums_s[:, pl.ds(pl.multiple_of(core * side, side), side)]
        sums_send[...] = sums_s[:, pl.ds(pl.multiple_of((1 - core) * side, side), side)]


def tail_kernel(n_res, where, *refs):
    grads = refs[:n_res]
    own_ref, weights, gain_w, out_ref = refs[n_res:]
    r = where[0]
    own = own_ref[...].reshape(-1, own_ref.shape[-1])
    total = jnp.zeros(own.shape, F32)
    for k in range(n_res):
        block = grads[k][...].reshape(own.shape[0], -1)
        total += dot(block, weights[jnp.bitwise_xor(r, k)])
    hat, inverse = norm_rows(own)
    g = total * gain_w[...]
    mean = jnp.mean(g, axis=-1, keepdims=True)
    cross = jnp.mean(g * hat, axis=-1, keepdims=True)
    out_ref[...] = (inverse * (g - mean - hat * cross)).astype(BF16).reshape(out_ref.shape)


def sums_kernel(n_res, width, where, mine, other, gain_ref, *outs):
    r, s = where[0], where[1]
    wide = outs[-1]
    outs = outs[:-1]
    side = mine.shape[2]
    core = jnp.bitwise_and(s, 1)
    here = pl.ds(pl.multiple_of(core * side, side), side)
    there = pl.ds(pl.multiple_of((1 - core) * side, side), side)
    gain = jnp.zeros((1, 2 * side), F32)
    for k in range(n_res):
        h = jnp.bitwise_xor(r, k)
        for ref, lanes in ((mine, here), (other, there)):
            block = ref[k].astype(F32)
            for n in range(5):
                rows = pl.ds(pl.multiple_of(h * width, width), width)
                wide[n, rows, lanes] = block[n * width : (n + 1) * width]
            wide[5, pl.ds(k, 1), lanes] = block[5 * width : 5 * width + 1] + block[5 * width + 1 : 5 * width + 2]
    gain = jnp.sum(wide[5, :n_res, :], axis=0, keepdims=True)
    gain_ref[...] = gain
    for n in range(4):
        outs[n][...] = jnp.transpose(wide[n])
    outs[4][...] = wide[4]


def whole(shape):
    return pl.BlockSpec(shape, lambda *_: (0,) * len(shape))


def by_head(
    n_res,
    n_seq,
    homolog_embedding,
    pair_input_rows,
    incoming_slope,
    rescale_factor,
    probe_weights,
    lookup_weights,
    content_weights,
    sigmoid_weights,
    final_projection,
    pair_bias_matrix,
):
    heads = pair_bias_matrix.shape[1]
    rows, own, channels = homolog_embedding.shape
    width = channels // heads
    total = own * n_res
    part = total // n_seq
    r, s = lax.axis_index("res"), lax.axis_index("seq")
    where = jnp.stack([r, s]).astype(jnp.int32)
    gain_row = rescale_factor.reshape(1, channels)

    both = jnp.stack([homolog_embedding, incoming_slope])
    tokens = [None] * n_res
    tokens[0] = both
    for k in range(2, n_res, 2):
        tokens[k] = exchange(both, "res", n_res, k)
    for k in range(0, n_res, 2):
        tokens[k + 1] = exchange(tokens[k], "res", n_res, 1)

    bias_local = jnp.einsum(
        "ijc,ch->hij", pair_input_rows, pair_bias_matrix, preferred_element_type=F32
    ).astype(BF16)
    bias_parts = [lax.dynamic_index_in_dim(bias_local, r ^ k, 0, keepdims=False) for k in range(n_res)]
    bias_parts = [bias_parts[0]] + [exchange(bias_parts[k], "res", n_res, k) for k in range(1, n_res)]
    bias_head = jnp.stack(bias_parts)
    biases = [bias_head] + [exchange(bias_head, "seq", n_seq, m) for m in range(1, n_seq)]

    by = [
        w.T.reshape(heads, 1, width, channels)
        for w in (probe_weights, lookup_weights, content_weights, sigmoid_weights)
    ]
    head_weights = jnp.concatenate(by, axis=1).reshape(heads, 4 * width, channels)
    out_weights = final_projection.reshape(heads, width, channels)

    token_spec = pl.BlockSpec((2, 1, own, channels), lambda i, w: (0, i, 0, 0))
    grad_spec = pl.BlockSpec((1, own, 4 * width), lambda i, w: (i, 0, 0))
    sum_rows = 5 * width + 16
    side = channels // 2
    span = min(total, 256)
    outs = pl.pallas_call(
        functools.partial(attention_kernel, n_res, n_seq, width, span),
        grid_spec=pltpu.PrefetchScalarGridSpec(
            num_scalar_prefetch=1,
            grid=(rows,),
            in_specs=[token_spec] * n_res
            + [whole((n_res, own, part))] * n_seq
            + [
                pl.BlockSpec((1, 4 * width, channels), lambda i, w: (w[0], 0, 0)),
                pl.BlockSpec((1, width, channels), lambda i, w: (w[0], 0, 0)),
                whole((1, channels)),
            ],
            out_specs=[grad_spec] * n_res
            + [whole((n_seq // 2, total, part))] * 2
            + [whole((sum_rows, side))] * 2,
            scratch_shapes=[
                pltpu.VMEM((total, channels), F32),
                pltpu.VMEM((total, channels), BF16),
                pltpu.VMEM((total, channels), BF16),
                pltpu.VMEM((total, total), BF16),
                pltpu.VMEM((total, total), F32),
                pltpu.VMEM((total, 4 * width), F32),
                pltpu.VMEM((sum_rows, channels), F32),
            ],
        ),
        out_shape=[jax.ShapeDtypeStruct((rows, own, 4 * width), BF16)] * n_res
        + [jax.ShapeDtypeStruct((n_seq // 2, total, part), F32)] * 2
        + [jax.ShapeDtypeStruct((sum_rows, side), F32)] * 2,
        compiler_params=pltpu.CompilerParams(vmem_limit_bytes=48 * 1024 * 1024),
        name="attention",
    )(where, *tokens, *biases, head_weights, out_weights, gain_row)
    grads, (pair_keep, pair_send, sums_keep, sums_send) = outs[:n_res], outs[n_res:]

    pair_sum = pair_keep + exchange(pair_send, "seq", n_seq, 1)
    sums = sums_keep + exchange(sums_send, "seq", n_seq, 1)
    step = 2
    while step < n_seq:
        half = pair_sum.shape[0] // 2
        pair_sum = pair_sum.reshape(half, 2, total, part)
        pair_sum = pair_sum[:, 0] + exchange(pair_sum[:, 1], "seq", n_seq, step)
        sums = sums + exchange(sums, "seq", n_seq, step)
        step *= 2
    pair_half = pair_sum.reshape(n_res, own, part).astype(BF16)
    sums_half = sums.astype(BF16)
    gain_at = 5 * width
    rest = (sums[gain_at : gain_at + 1] - sums_half[gain_at : gain_at + 1].astype(F32)).astype(BF16)
    sums_half = jnp.concatenate([sums_half[: gain_at + 1], rest, sums_half[gain_at + 2 :]], axis=0)

    pair_parts = [lax.dynamic_index_in_dim(pair_half, r ^ k, 0, keepdims=False) for k in range(n_res)]
    pair_parts = [pair_parts[0]] + [exchange(pair_parts[k], "res", n_res, k) for k in range(1, n_res)]
    grads = [grads[0]] + [exchange(grads[k], "res", n_res, k) for k in range(1, n_res)]
    sums_all = jnp.stack([sums_half] + [exchange(sums_half, "res", n_res, k) for k in range(1, n_res)])
    sums_other = exchange(sums_all, "seq", n_seq, 1)

    dbias_own = jnp.stack([lax.dynamic_index_in_dim(jnp.stack(pair_parts), r ^ h, 0, keepdims=False) for h in range(n_res)])
    pair_input_gradient = jnp.einsum(
        "hij,ch->ijc", dbias_own, pair_bias_matrix, preferred_element_type=F32
    ).astype(BF16)
    part_bias = jnp.einsum("ijc,hij->ch", pair_input_rows, dbias_own, preferred_element_type=F32)
    for axis, size in (("seq", n_seq), ("res", n_res)):
        step = 1
        while step < size:
            part_bias = part_bias + exchange(part_bias, axis, size, step)
            step *= 2

    alignment_rows_gradient = pl.pallas_call(
        functools.partial(tail_kernel, n_res),
        grid_spec=pltpu.PrefetchScalarGridSpec(
            num_scalar_prefetch=1,
            grid=(rows,),
            in_specs=[grad_spec] * n_res
            + [
                pl.BlockSpec((1, own, channels), lambda i, w: (i, 0, 0)),
                whole((heads, 4 * width, channels)),
                whole((1, channels)),
            ],
            out_specs=pl.BlockSpec((1, own, channels), lambda i, w: (i, 0, 0)),
        ),
        out_shape=jax.ShapeDtypeStruct(homolog_embedding.shape, BF16),
        compiler_params=pltpu.CompilerParams(vmem_limit_bytes=32 * 1024 * 1024),
        name="tail",
    )(where, *grads, homolog_embedding, head_weights, gain_row)

    square = jax.ShapeDtypeStruct((channels, channels), F32)
    gain, dq, dk, dv, dg, dout = pl.pallas_call(
        functools.partial(sums_kernel, n_res, width),
        grid_spec=pltpu.PrefetchScalarGridSpec(
            num_scalar_prefetch=1,
            grid=(1,),
            in_specs=[whole((n_res, sum_rows, side))] * 2,
            out_specs=[whole((1, channels))] + [whole((channels, channels))] * 5,
            scratch_shapes=[pltpu.VMEM((6, channels, channels), F32)],
        ),
        out_shape=[jax.ShapeDtypeStruct((1, channels), F32)] + [square] * 5,
        compiler_params=pltpu.CompilerParams(vmem_limit_bytes=32 * 1024 * 1024),
        name="sums",
    )(where, sums_all, sums_other)
    return (
        alignment_rows_gradient,
        pair_input_gradient,
        gain.reshape(channels),
        dq,
        dk,
        dv,
        dg,
        dout,
        part_bias,
    )


def layer_norm_rows(alignment_block):
    content_vectors = alignment_block.astype(jnp.float32)
    centered = content_vectors - jnp.mean(content_vectors, axis=-1, keepdims=True)
    inverse_deviation = lax.rsqrt(jnp.mean(centered * centered, axis=-1, keepdims=True) + 1e-05)
    return (centered * inverse_deviation, inverse_deviation)


def row_backward(bias_full, head_count, dbias_total, row_inputs):
    probe_vectors, keys_row, values_row, gate_row, derivative_modulated = row_inputs
    query_total, channel_width = probe_vectors.shape
    key_count = keys_row.shape[0]
    head_width = channel_width // head_count
    softmax_scale = 1.0 / math.sqrt(head_width)
    query_heads = probe_vectors.reshape(query_total, head_count, head_width)
    key_heads = keys_row.reshape(key_count, head_count, head_width)
    value_heads = values_row.reshape(key_count, head_count, head_width)
    scores = (
        jnp.einsum("ihd,jhd->hij", query_heads, key_heads, preferred_element_type=jnp.float32)
        * softmax_scale
    )
    scores = scores + bias_full.astype(jnp.float32)
    weights_soft = jax.nn.softmax(scores, axis=-1)
    weights_half = weights_soft.astype(jnp.bfloat16)
    attended = jnp.einsum(
        "hij,jhd->ihd", weights_half, value_heads, preferred_element_type=jnp.float32
    ).reshape(query_total, channel_width)
    modulated_result = (gate_row * attended).astype(jnp.bfloat16)
    grad_attended = (derivative_modulated * gate_row).astype(jnp.bfloat16)
    derivative_logits_sigmoid = (
        derivative_modulated * attended * gate_row * (1.0 - gate_row)
    ).astype(jnp.bfloat16)
    grad_heads = grad_attended.reshape(query_total, head_count, head_width)
    grad_weights = jnp.einsum(
        "ihd,jhd->hij", grad_heads, value_heads, preferred_element_type=jnp.float32
    )
    row_inner = jnp.sum(weights_soft * grad_weights, axis=-1, keepdims=True)
    grad_scores = weights_soft * (grad_weights - row_inner)
    scores_half = grad_scores.astype(jnp.bfloat16)
    derivative_probe_weights = (
        jnp.einsum("hij,jhd->ihd", scores_half, key_heads, preferred_element_type=jnp.float32)
        * softmax_scale
    ).astype(jnp.bfloat16)
    derivative_lookup_weights = (
        jnp.einsum("hij,ihd->jhd", scores_half, query_heads, preferred_element_type=jnp.float32)
        * softmax_scale
    )
    derivative_content_weights = jnp.einsum(
        "hij,ihd->jhd", weights_half, grad_heads, preferred_element_type=jnp.float32
    )
    outputs = (
        modulated_result,
        derivative_logits_sigmoid,
        derivative_probe_weights.reshape(query_total, channel_width),
        derivative_lookup_weights.reshape(key_count, channel_width),
        derivative_content_weights.reshape(key_count, channel_width),
    )
    return (dbias_total + grad_scores, outputs)


def body(
    homolog_embedding,
    pair_input_rows,
    incoming_slope,
    rescale_factor,
    probe_weights,
    lookup_weights,
    content_weights,
    sigmoid_weights,
    final_projection,
    pair_bias_matrix,
):
    highest = lax.Precision.HIGHEST
    head_count = pair_bias_matrix.shape[1]
    row_total, query_total, channel_width = homolog_embedding.shape
    standardized_rows, inverse_deviation = layer_norm_rows(homolog_embedding)
    rescaled_embedding = (standardized_rows * rescale_factor).astype(jnp.bfloat16)
    rescaled_plain = rescaled_embedding.reshape(-1, channel_width)
    probe_vectors = (
        jnp.dot(rescaled_plain, probe_weights, preferred_element_type=jnp.float32)
        .astype(jnp.bfloat16)
        .reshape(row_total, query_total, channel_width)
    )
    sigmoid_factors = jax.nn.sigmoid(
        jnp.dot(rescaled_plain, sigmoid_weights, preferred_element_type=jnp.float32)
    ).reshape(row_total, query_total, channel_width)
    incoming_slope_plain = incoming_slope.reshape(-1, channel_width)
    derivative_modulated = jnp.dot(
        incoming_slope_plain, final_projection.T, preferred_element_type=jnp.float32
    ).reshape(row_total, query_total, channel_width)
    bias_local = jnp.einsum(
        "ijc,ch->hij", pair_input_rows, pair_bias_matrix, preferred_element_type=jnp.float32
    ).astype(jnp.bfloat16)
    bias_full = lax.all_gather(bias_local, "seq", axis=2, tiled=True)
    normed_all = lax.all_gather(rescaled_embedding, "res", axis=1, tiled=True)
    key_count = normed_all.shape[1]
    all_flat = normed_all.reshape(-1, channel_width)
    lookup_vectors = (
        jnp.dot(all_flat, lookup_weights, preferred_element_type=jnp.float32)
        .astype(jnp.bfloat16)
        .reshape(row_total, key_count, channel_width)
    )
    content_vectors = (
        jnp.dot(all_flat, content_weights, preferred_element_type=jnp.float32)
        .astype(jnp.bfloat16)
        .reshape(row_total, key_count, channel_width)
    )
    dbias_init = jnp.zeros(bias_full.shape, jnp.float32)
    dbias_local, row_results = lax.scan(
        functools.partial(row_backward, bias_full, head_count),
        dbias_init,
        (probe_vectors, lookup_vectors, content_vectors, sigmoid_factors, derivative_modulated),
    )
    (
        modulated_result,
        derivative_logits_sigmoid,
        derivative_probe_weights,
        derivative_lookup_weights,
        derivative_content_weights,
    ) = row_results
    key_weight_wide = lookup_weights.astype(jnp.float32)
    value_weight_wide = content_weights.astype(jnp.float32)
    lookup_plain = derivative_lookup_weights.reshape(-1, channel_width)
    content_plain = derivative_content_weights.reshape(-1, channel_width)
    key_term = (
        jnp.dot(lookup_plain, key_weight_wide.T, precision=highest)
        + jnp.dot(content_plain, value_weight_wide.T, precision=highest)
    ).reshape(row_total, -1, channel_width)
    grad_from_keys = lax.psum_scatter(key_term, "res", scatter_dimension=1, tiled=True).reshape(
        -1, channel_width
    )
    all_wide = all_flat.astype(jnp.float32)
    part_key = jnp.dot(all_wide.T, lookup_plain, precision=highest)
    part_value = jnp.dot(all_wide.T, content_plain, precision=highest)
    probe_plain = derivative_probe_weights.reshape(-1, channel_width)
    sigmoid_factor_plain = derivative_logits_sigmoid.reshape(-1, channel_width)
    part_query = jnp.dot(rescaled_plain.T, probe_plain, preferred_element_type=jnp.float32)
    part_gate = jnp.dot(rescaled_plain.T, sigmoid_factor_plain, preferred_element_type=jnp.float32)
    part_out = jnp.dot(
        modulated_result.reshape(-1, channel_width).T,
        incoming_slope_plain,
        preferred_element_type=jnp.float32,
    )
    derivative_rescaled = (
        jnp.dot(probe_plain, probe_weights.T, preferred_element_type=jnp.float32)
        + jnp.dot(sigmoid_factor_plain, sigmoid_weights.T, preferred_element_type=jnp.float32)
        + grad_from_keys
    )
    derivative_rescaled = derivative_rescaled.reshape(row_total, query_total, channel_width)
    part_gain = jnp.sum(derivative_rescaled * standardized_rows, axis=(0, 1))
    centered_scaled_gradient = derivative_rescaled * rescale_factor
    alignment_rows_gradient = (
        inverse_deviation
        * (
            centered_scaled_gradient
            - jnp.mean(centered_scaled_gradient, axis=-1, keepdims=True)
            - standardized_rows
            * jnp.mean(centered_scaled_gradient * standardized_rows, axis=-1, keepdims=True)
        )
    ).astype(jnp.bfloat16)
    dbias_own = lax.psum_scatter(dbias_local, "seq", scatter_dimension=2, tiled=True).astype(
        jnp.bfloat16
    )
    pair_input_gradient = jnp.einsum(
        "hij,ch->ijc", dbias_own, pair_bias_matrix, preferred_element_type=jnp.float32
    ).astype(jnp.bfloat16)
    part_bias = jnp.einsum(
        "ijc,hij->ch", pair_input_rows, dbias_own, preferred_element_type=jnp.float32
    )
    totals = lax.psum(
        (part_gain, part_query, part_key, part_value, part_gate, part_out, part_bias),
        ("seq", "res"),
    )
    return (
        alignment_rows_gradient,
        pair_input_gradient,
        totals[0],
        totals[1],
        totals[2],
        totals[3],
        totals[4],
        totals[5],
        totals[6],
    )


def solution(mesh):
    in_specs = (
        P("seq", "res", None),
        P("res", "seq", None),
        P("seq", "res", None),
        P(),
        P(),
        P(),
        P(),
        P(),
        P(),
        P(),
    )
    out_specs = (P("seq", "res", None), P("res", "seq", None), P(), P(), P(), P(), P(), P(), P())
    n_res, n_seq = mesh.shape["res"], mesh.shape["seq"]

    def run(*args):
        if n_res == args[-1].shape[1] and n_res & (n_res - 1) == 0 and n_seq > 1 and n_seq & (n_seq - 1) == 0:
            return by_head(n_res, n_seq, *args)
        return body(*args)

    return jax.shard_map(run, mesh=mesh, in_specs=in_specs, out_specs=out_specs, check_vma=False)
```

```python
import functools
import math

import jax
import jax.numpy as jnp
from jax import lax
from jax.experimental import pallas as pl
from jax.experimental.pallas import tpu as pltpu
from jax.sharding import PartitionSpec as P

F32 = jnp.float32
BF16 = jnp.bfloat16


def exchange(value, axis, size, offset):
    return lax.ppermute(value, axis, [(i, i ^ offset) for i in range(size)])


def dot(a, b, dims=((1,), (0,))):
    return lax.dot_general(a, b, (dims, ((), ())), preferred_element_type=F32)


def norm_rows(block):
    wide = block.astype(F32)
    centered = wide - jnp.mean(wide, axis=-1, keepdims=True)
    inverse = lax.rsqrt(jnp.mean(centered * centered, axis=-1, keepdims=True) + 1e-05)
    return centered * inverse, inverse


def place(r, k, own):
    return pl.ds(pl.multiple_of(jnp.bitwise_xor(r, k) * own, own), own)


def ready_kernel(own_ref, slope_ref, bias_ref, gate_w, out_w, gain_w, out_ref):
    heads, bias_rows, lanes = bias_ref.shape
    channels = gain_w.shape[1]
    width = channels // heads
    hat, _ = norm_rows(own_ref[...].reshape(-1, channels))
    normed = (hat * gain_w[...]).astype(BF16)
    gate = jax.nn.sigmoid(dot(normed, gate_w[...]))
    dgated = dot(slope_ref[...].reshape(-1, channels), out_w[...], ((1,), (1,)))
    datt = jnp.transpose((dgated * gate).astype(BF16).astype(F32)).astype(BF16)
    out_ref[:, :bias_rows, :] = bias_ref[...]
    for h in range(heads):
        for n in range(datt.shape[1] // lanes):
            at = bias_rows + n * width
            out_ref[h, at : at + width, :] = datt[h * width : (h + 1) * width, n * lanes : (n + 1) * lanes]


def attention_kernel(n_res, n_seq, width, span, where, *refs):
    tokens = refs[:n_res]
    biases, datts, head_w, gain_w, flow_ref, keep_ref, send_ref = refs[n_res:][:7]
    normed_s, datt_s, bias_s, dbias_s = refs[-4:]
    row, last = pl.program_id(0), pl.num_programs(0) - 1
    r, s = where[0], where[1]
    own = tokens[0].shape[1]
    total = own * n_res
    part = total // n_seq
    scale = 1.0 / math.sqrt(width)

    @pl.when(row == 0)
    def _():
        for m in range(n_seq):
            bias_s[:, m * part : (m + 1) * part] = biases[m]
        for k in range(n_res):
            for n in range(datts.shape[1] // width):
                block = jnp.transpose(datts[k, n * width : (n + 1) * width, :].astype(F32)).astype(BF16)
                for m in range(block.shape[0] // own):
                    at = n * (block.shape[0] // own) + m
                    datt_s[at, k * own : (k + 1) * own, :] = block[m * own : (m + 1) * own]
        dbias_s[...] = jnp.zeros_like(dbias_s)

    for k in range(n_res):
        hat, _ = norm_rows(tokens[k][0])
        normed_s[place(r, k, own), :] = (hat * gain_w[...]).astype(BF16)

    normed = normed_s[...]
    weights = head_w[0]
    wq, wk, wv = (weights[n * width : (n + 1) * width] for n in range(3))
    rows = ((1,), (1,))
    q = dot(normed, wq, rows).astype(BF16)
    k_ = dot(normed, wk, rows).astype(BF16)
    v = dot(normed, wv, rows).astype(BF16)
    datt = datt_s[row]
    q_t, k_t, v_t, datt_t = (jnp.transpose(x) for x in (q, k_, v, datt))

    gk_t = jnp.zeros((width, total), F32)
    gv_t = jnp.zeros((width, total), F32)
    gqs, atts = [], []
    for c in range(total // span):
        lo, hi = c * span, (c + 1) * span
        scores = dot(q[lo:hi], k_t) * scale + bias_s[lo:hi, :].astype(F32)
        top = jnp.max(scores, axis=-1, keepdims=True)
        e = jnp.exp(scores - top)
        soft = e * (1.0 / jnp.sum(e, axis=-1, keepdims=True))
        half = soft.astype(BF16)
        atts.append(dot(half, v))
        gv_t += dot(datt_t[:, lo:hi], half)
        dsoft = dot(datt[lo:hi], v_t)
        inner = jnp.sum(soft * dsoft, axis=-1, keepdims=True)
        dscores = soft * (dsoft - inner)
        dbias_s[lo:hi, :] += dscores
        dhalf = dscores.astype(BF16)
        gqs.append(dot(dhalf, k_) * scale)
        gk_t += dot(q_t[:, lo:hi], dhalf)
    flow_ref[0, :width, :] = jnp.transpose(jnp.concatenate(gqs, axis=0))
    flow_ref[0, width : 2 * width, :] = gk_t * scale
    flow_ref[0, 2 * width : 3 * width, :] = gv_t
    flow_ref[0, 3 * width :, :] = jnp.transpose(jnp.concatenate(atts, axis=0))

    @pl.when(row == last)
    def _():
        for m in range(n_seq):
            lane = pl.multiple_of(jnp.bitwise_xor(s, m) * part, part)
            at = m // 2 * total
            (send_ref if m % 2 else keep_ref)[at : at + total, :] = dbias_s[:, pl.ds(lane, part)]


def gradient_kernel(n_res, width, where, *refs):
    tokens, slopes = refs[:n_res], refs[n_res : n_res + n_res // 2]
    refs = refs[n_res + n_res // 2 :]
    flow_ref, head_w, out_w, gain_w, pair_keep, pair_send, grad_ref, keep_ref, send_ref = refs[:9]
    hat_s, normed_s, slope_s, sums_s = refs[-4:]
    row, last = pl.program_id(0), pl.num_programs(0) - 1
    r, s = where[0], where[1]
    own, channels = tokens[0].shape[1:]

    @pl.when(row == 0)
    def _():
        sums_s[...] = jnp.zeros_like(sums_s)

    for k in range(n_res):
        hat, _ = norm_rows(tokens[k][0])
        hat_s[place(r, k, own), :] = hat
        normed_s[place(r, k, own), :] = (hat * gain_w[...]).astype(BF16)
        slope_s[place(r, k, own), :] = slopes[k // 2][k % 2, 0]
    normed = normed_s[...]
    slope = slope_s[...]
    weights = head_w[0]
    rows = ((1,), (1,))
    gate = jax.nn.sigmoid(dot(weights[3 * width :], normed, rows))
    dgated = dot(out_w[0], slope, rows)
    att = flow_ref[0, 3 * width :, :]
    gated = (gate * att).astype(BF16)
    dgate = dgated * att * gate * (1.0 - gate)
    grad_t = jnp.concatenate([flow_ref[0, : 3 * width, :], dgate], axis=0)
    high_t = grad_t.astype(BF16)
    at = lax.broadcasted_iota(jnp.int32, grad_t.shape, 0)
    wide = (at >= width) & (at < 3 * width)
    low_t = jnp.where(wide, grad_t - high_t.astype(F32), 0.0).astype(BF16)
    high = jnp.transpose(grad_t).astype(BF16)
    low = jnp.transpose(low_t.astype(F32)).astype(BF16)
    sums_s[: 4 * width, :] += dot(high_t, normed) + dot(low_t, normed)
    sums_s[4 * width : 5 * width, :] += dot(gated, slope)
    grad_normed = dot(high, weights) + dot(low, weights)
    sums_s[5 * width : 5 * width + 1, :] += jnp.sum(grad_normed * hat_s[...], axis=0, keepdims=True)
    for k in range(n_res):
        grad_ref[k, 0] = high[k * own : (k + 1) * own]

    @pl.when(row == last)
    def _():
        side = channels // 2
        core = jnp.bitwise_and(s, 1)
        at = pair_keep.shape[0]
        keep_ref[:at, :] = pair_keep[...]
        send_ref[:at, :] = pair_send[...]
        keep_ref[at:, :] = sums_s[:, pl.ds(pl.multiple_of(core * side, side), side)]
        send_ref[at:, :] = sums_s[:, pl.ds(pl.multiple_of((1 - core) * side, side), side)]


def weights_kernel(width, *refs):
    out = refs[-1]
    for n, ref in enumerate(refs[:-1]):
        flipped = jnp.transpose(ref[...].astype(F32)).astype(BF16)
        for h in range(out.shape[0]):
            out[h, n * width : (n + 1) * width, :] = flipped[h * width : (h + 1) * width]


def back_kernel(n_res, own, gain_at, where, keep, come, *outs):
    total = n_res * own
    sums = keep[total:, :] + come[total:, :]
    half = sums.astype(BF16)
    rest = (sums - half.astype(F32))[gain_at:].astype(BF16)
    tail = jnp.concatenate([half[:gain_at], jnp.concatenate([half[gain_at:], rest], axis=0)], axis=0)
    for k in range(n_res):
        at = place(where[0], k, own)
        outs[k][:own, :] = (keep[at, :] + come[at, :]).astype(BF16)
        outs[k][own:, :] = tail


def pair_kernel(n_res, where, *refs):
    blocks = refs[:n_res]
    rows_ref, out_ref, grad_ref, sums_ref, wide = refs[n_res:]
    own = grad_ref.shape[1]
    for k in range(n_res):
        h = jnp.bitwise_xor(where[0], k)
        grad_ref[h] = blocks[k][:own, :]
        wide[h] = blocks[k][:own, :].astype(F32)
        sums_ref[h] = blocks[k][own:, :]
    total = jnp.zeros(out_ref.shape[1:], F32)
    for i in range(own):
        total += dot(wide[:, i, :].astype(BF16), rows_ref[i])
    for n in range(out_ref.shape[0]):
        out_ref[n] = total


def tail_kernel(grads, own_ref, weights, gain_w, out_ref):
    own = own_ref[0]
    total = jnp.zeros(own.shape, F32)
    for h in range(grads.shape[0]):
        total += dot(grads[h, 0], weights[h])
    hat, inverse = norm_rows(own)
    g = total * gain_w[...]
    mean = jnp.mean(g, axis=-1, keepdims=True)
    cross = jnp.mean(g * hat, axis=-1, keepdims=True)
    out_ref[0] = (inverse * (g - mean - hat * cross)).astype(BF16)


def sums_kernel(width, where, mine, other, gain_ref, *refs):
    outs, wide = refs[:-1], refs[-1]
    heads, _, side = mine.shape
    core = jnp.bitwise_and(where[1], 1)
    here = pl.ds(pl.multiple_of(core * side, side), side)
    there = pl.ds(pl.multiple_of((1 - core) * side, side), side)
    for ref, lanes in ((mine, here), (other, there)):
        extra = jnp.zeros((1, side), F32)
        for h in range(heads):
            block = ref[h].astype(F32)
            for n in range(5):
                wide[n, h * width : (h + 1) * width, lanes] = block[n * width : (n + 1) * width]
            extra += block[5 * width : 5 * width + 1] + block[5 * width + 8 : 5 * width + 9]
        gain_ref[:, lanes] = extra
    for n in range(4):
        outs[n][...] = jnp.transpose(wide[n])
    outs[4][...] = wide[4]


def whole(shape):
    return pl.BlockSpec(shape, lambda *_: (0,) * len(shape))


def by_head(
    n_res,
    n_seq,
    homolog_embedding,
    pair_input_rows,
    incoming_slope,
    rescale_factor,
    probe_weights,
    lookup_weights,
    content_weights,
    sigmoid_weights,
    final_projection,
    pair_bias_matrix,
):
    heads = pair_bias_matrix.shape[1]
    rows, own, channels = homolog_embedding.shape
    width = channels // heads
    total = own * n_res
    part = total // n_seq
    r, s = lax.axis_index("res"), lax.axis_index("seq")
    where = jnp.stack([r, s]).astype(jnp.int32)
    gain_row = rescale_factor.reshape(1, channels)

    def params(mib=48):
        return pltpu.CompilerParams(vmem_limit_bytes=mib * 1024 * 1024)

    bias_local = jnp.einsum(
        "ijc,ch->hij", pair_input_rows, pair_bias_matrix, preferred_element_type=F32
    ).astype(BF16)
    flat = rows * own // part * width
    ready = pl.pallas_call(
        ready_kernel,
        out_shape=jax.ShapeDtypeStruct((heads, own + flat, part), BF16),
        compiler_params=params(),
        name="ready",
    )(homolog_embedding, incoming_slope, bias_local, sigmoid_weights, final_projection, gain_row)
    ready = lax.all_to_all(ready, "res", 0, 0, tiled=True)
    slope_pair = jnp.stack([incoming_slope, exchange(incoming_slope, "res", n_res, 1)])
    ready, embedding = lax.optimization_barrier((ready, homolog_embedding))
    datts = ready[:, own:]
    tokens = [embedding] + [exchange(embedding, "res", n_res, k) for k in range(1, n_res) if k == 1 or k % 2 == 0]
    bias_all = lax.all_gather(ready[:, :own].reshape(total, part), "seq", axis=0)
    bias_all, slope_pair, *tokens = lax.optimization_barrier((bias_all, slope_pair, *tokens))
    tokens = tokens[:2] + [b for block in tokens[2:] for b in (block, exchange(block, "res", n_res, 1))]
    slopes = [slope_pair] + [exchange(slope_pair, "res", n_res, k) for k in range(2, n_res, 2)]

    head_weights = pl.pallas_call(
        functools.partial(weights_kernel, width),
        out_shape=jax.ShapeDtypeStruct((heads, 4 * width, channels), BF16),
        compiler_params=params(),
        name="weights",
    )(probe_weights, lookup_weights, content_weights, sigmoid_weights)
    out_weights = final_projection.reshape(heads, width, channels)

    token_spec = pl.BlockSpec((1, own, channels), lambda i, w: (i, 0, 0))
    flow_spec = pl.BlockSpec((1, 4 * width, total), lambda i, w: (i, 0, 0))
    weight_spec = pl.BlockSpec((1, 4 * width, channels), lambda i, w: (w[0], 0, 0))
    out_spec = pl.BlockSpec((1, width, channels), lambda i, w: (w[0], 0, 0))
    sum_rows = 5 * width + 8
    side = channels // 2
    pair_rows = n_seq // 2 * total
    merged = jax.ShapeDtypeStruct((pair_rows + sum_rows, side), F32)
    flow, pair_keep, pair_send = pl.pallas_call(
        functools.partial(attention_kernel, n_res, n_seq, width, min(total, 256)),
        grid_spec=pltpu.PrefetchScalarGridSpec(
            num_scalar_prefetch=1,
            grid=(rows,),
            in_specs=[token_spec] * n_res
            + [whole((n_seq, total, part)), whole((n_res, flat, part)), weight_spec, whole((1, channels))],
            out_specs=[flow_spec] + [whole((pair_rows, part))] * 2,
            scratch_shapes=[
                pltpu.VMEM((total, channels), BF16),
                pltpu.VMEM((rows, total, width), BF16),
                pltpu.VMEM((total, total), BF16),
                pltpu.VMEM((total, total), F32),
            ],
        ),
        out_shape=[jax.ShapeDtypeStruct((rows, 4 * width, total), F32)]
        + [jax.ShapeDtypeStruct((pair_rows, part), F32)] * 2,
        compiler_params=params(60),
        name="attention",
    )(where, *tokens, bias_all, datts, head_weights, gain_row)

    grads, keep, send = pl.pallas_call(
        functools.partial(gradient_kernel, n_res, width),
        grid_spec=pltpu.PrefetchScalarGridSpec(
            num_scalar_prefetch=1,
            grid=(rows,),
            in_specs=[token_spec] * n_res
            + [pl.BlockSpec((2, 1, own, channels), lambda i, w: (0, i, 0, 0))] * (n_res // 2)
            + [flow_spec, weight_spec, out_spec, whole((1, channels))]
            + [whole((pair_rows, part))] * 2,
            out_specs=[pl.BlockSpec((n_res, 1, own, 4 * width), lambda i, w: (0, i, 0, 0))]
            + [whole(merged.shape)] * 2,
            scratch_shapes=[
                pltpu.VMEM((total, channels), F32),
                pltpu.VMEM((total, channels), BF16),
                pltpu.VMEM((total, channels), BF16),
                pltpu.VMEM((sum_rows, channels), F32),
            ],
        ),
        out_shape=[jax.ShapeDtypeStruct((n_res, rows, own, 4 * width), BF16)]
        + [merged, merged],
        compiler_params=params(60),
        name="gradients",
    )(where, *tokens, *slopes, flow, head_weights, out_weights, gain_row, pair_keep, pair_send)

    grads = lax.all_to_all(grads, "res", 0, 0, tiled=True)
    step = 1
    while True:
        come = exchange(send, "seq", n_seq, step)
        step *= 2
        if step == n_seq:
            break
        summed = keep + come
        half = (summed.shape[0] - sum_rows) // 2
        keep = jnp.concatenate([summed[:half], summed[2 * half :]], axis=0)
        send = summed[half:]
    come, grads = lax.optimization_barrier((come, grads))
    back_rows = own + sum_rows + 8
    backs = pl.pallas_call(
        functools.partial(back_kernel, n_res, own, 5 * width),
        grid_spec=pltpu.PrefetchScalarGridSpec(
            num_scalar_prefetch=1,
            grid=(1,),
            in_specs=[whole(keep.shape)] * 2,
            out_specs=[whole((back_rows, side))] * n_res,
        ),
        out_shape=[jax.ShapeDtypeStruct((back_rows, side), BF16)] * n_res,
        compiler_params=params(),
        name="back",
    )(where, keep, come)
    backs = [backs[0]] + [exchange(backs[k], "res", n_res, k) for k in range(1, n_res)]
    part_bias, dbias_own, sums = pl.pallas_call(
        functools.partial(pair_kernel, n_res),
        grid_spec=pltpu.PrefetchScalarGridSpec(
            num_scalar_prefetch=1,
            grid=(1,),
            in_specs=[whole((back_rows, side))] * n_res + [whole(pair_input_rows.shape)],
            out_specs=[whole((n_seq * n_res, heads, pair_input_rows.shape[2])), whole((heads, own, part)), whole((heads, sum_rows + 8, side))],
            scratch_shapes=[pltpu.VMEM((n_res, own, part), F32)],
        ),
        out_shape=[
            jax.ShapeDtypeStruct((n_seq * n_res, heads, pair_input_rows.shape[2]), F32),
            jax.ShapeDtypeStruct((heads, own, part), BF16),
            jax.ShapeDtypeStruct((heads, sum_rows + 8, side), BF16),
        ],
        compiler_params=params(),
        name="pair",
    )(where, *backs, pair_input_rows)
    part_bias, own_rows = lax.optimization_barrier((part_bias, homolog_embedding))
    other = exchange(sums, "seq", n_seq, 1)
    part_bias = lax.all_to_all(part_bias, ("seq", "res"), 0, 0, tiled=True)
    pair_input_gradient = jnp.einsum(
        "hij,ch->ijc", dbias_own, pair_bias_matrix, preferred_element_type=F32
    ).astype(BF16)

    alignment_rows_gradient = pl.pallas_call(
        tail_kernel,
        grid=(rows,),
        in_specs=[
            pl.BlockSpec((n_res, 1, own, 4 * width), lambda i: (0, i, 0, 0)),
            pl.BlockSpec((1, own, channels), lambda i: (i, 0, 0)),
            whole((heads, 4 * width, channels)),
            whole((1, channels)),
        ],
        out_specs=pl.BlockSpec((1, own, channels), lambda i: (i, 0, 0)),
        out_shape=jax.ShapeDtypeStruct(homolog_embedding.shape, BF16),
        compiler_params=params(),
        name="tail",
    )(grads, own_rows, head_weights, gain_row)

    square = jax.ShapeDtypeStruct((channels, channels), F32)
    gain, *weight_sums = pl.pallas_call(
        functools.partial(sums_kernel, width),
        grid_spec=pltpu.PrefetchScalarGridSpec(
            num_scalar_prefetch=1,
            grid=(1,),
            in_specs=[whole(sums.shape)] * 2,
            out_specs=[whole((1, channels))] + [whole((channels, channels))] * 5,
            scratch_shapes=[pltpu.VMEM((5, channels, channels), F32)],
        ),
        out_shape=[jax.ShapeDtypeStruct((1, channels), F32)] + [square] * 5,
        compiler_params=params(),
        name="sums",
    )(where, sums, other)
    part_bias, gain = lax.optimization_barrier((part_bias, gain))
    part_bias = part_bias.sum(axis=0)
    return (alignment_rows_gradient, pair_input_gradient, gain.reshape(channels), *weight_sums, part_bias.T)


def layer_norm_rows(alignment_block):
    content_vectors = alignment_block.astype(jnp.float32)
    centered = content_vectors - jnp.mean(content_vectors, axis=-1, keepdims=True)
    inverse_deviation = lax.rsqrt(jnp.mean(centered * centered, axis=-1, keepdims=True) + 1e-05)
    return (centered * inverse_deviation, inverse_deviation)


def row_backward(bias_full, head_count, dbias_total, row_inputs):
    probe_vectors, keys_row, values_row, gate_row, derivative_modulated = row_inputs
    query_total, channel_width = probe_vectors.shape
    key_count = keys_row.shape[0]
    head_width = channel_width // head_count
    softmax_scale = 1.0 / math.sqrt(head_width)
    query_heads = probe_vectors.reshape(query_total, head_count, head_width)
    key_heads = keys_row.reshape(key_count, head_count, head_width)
    value_heads = values_row.reshape(key_count, head_count, head_width)
    scores = (
        jnp.einsum("ihd,jhd->hij", query_heads, key_heads, preferred_element_type=jnp.float32)
        * softmax_scale
    )
    scores = scores + bias_full.astype(jnp.float32)
    weights_soft = jax.nn.softmax(scores, axis=-1)
    weights_half = weights_soft.astype(jnp.bfloat16)
    attended = jnp.einsum(
        "hij,jhd->ihd", weights_half, value_heads, preferred_element_type=jnp.float32
    ).reshape(query_total, channel_width)
    modulated_result = (gate_row * attended).astype(jnp.bfloat16)
    grad_attended = (derivative_modulated * gate_row).astype(jnp.bfloat16)
    derivative_logits_sigmoid = (
        derivative_modulated * attended * gate_row * (1.0 - gate_row)
    ).astype(jnp.bfloat16)
    grad_heads = grad_attended.reshape(query_total, head_count, head_width)
    grad_weights = jnp.einsum(
        "ihd,jhd->hij", grad_heads, value_heads, preferred_element_type=jnp.float32
    )
    row_inner = jnp.sum(weights_soft * grad_weights, axis=-1, keepdims=True)
    grad_scores = weights_soft * (grad_weights - row_inner)
    scores_half = grad_scores.astype(jnp.bfloat16)
    derivative_probe_weights = (
        jnp.einsum("hij,jhd->ihd", scores_half, key_heads, preferred_element_type=jnp.float32)
        * softmax_scale
    ).astype(jnp.bfloat16)
    derivative_lookup_weights = (
        jnp.einsum("hij,ihd->jhd", scores_half, query_heads, preferred_element_type=jnp.float32)
        * softmax_scale
    )
    derivative_content_weights = jnp.einsum(
        "hij,ihd->jhd", weights_half, grad_heads, preferred_element_type=jnp.float32
    )
    outputs = (
        modulated_result,
        derivative_logits_sigmoid,
        derivative_probe_weights.reshape(query_total, channel_width),
        derivative_lookup_weights.reshape(key_count, channel_width),
        derivative_content_weights.reshape(key_count, channel_width),
    )
    return (dbias_total + grad_scores, outputs)


def body(
    homolog_embedding,
    pair_input_rows,
    incoming_slope,
    rescale_factor,
    probe_weights,
    lookup_weights,
    content_weights,
    sigmoid_weights,
    final_projection,
    pair_bias_matrix,
):
    highest = lax.Precision.HIGHEST
    head_count = pair_bias_matrix.shape[1]
    row_total, query_total, channel_width = homolog_embedding.shape
    standardized_rows, inverse_deviation = layer_norm_rows(homolog_embedding)
    rescaled_embedding = (standardized_rows * rescale_factor).astype(jnp.bfloat16)
    rescaled_plain = rescaled_embedding.reshape(-1, channel_width)
    probe_vectors = (
        jnp.dot(rescaled_plain, probe_weights, preferred_element_type=jnp.float32)
        .astype(jnp.bfloat16)
        .reshape(row_total, query_total, channel_width)
    )
    sigmoid_factors = jax.nn.sigmoid(
        jnp.dot(rescaled_plain, sigmoid_weights, preferred_element_type=jnp.float32)
    ).reshape(row_total, query_total, channel_width)
    incoming_slope_plain = incoming_slope.reshape(-1, channel_width)
    derivative_modulated = jnp.dot(
        incoming_slope_plain, final_projection.T, preferred_element_type=jnp.float32
    ).reshape(row_total, query_total, channel_width)
    bias_local = jnp.einsum(
        "ijc,ch->hij", pair_input_rows, pair_bias_matrix, preferred_element_type=jnp.float32
    ).astype(jnp.bfloat16)
    bias_full = lax.all_gather(bias_local, "seq", axis=2, tiled=True)
    normed_all = lax.all_gather(rescaled_embedding, "res", axis=1, tiled=True)
    key_count = normed_all.shape[1]
    all_flat = normed_all.reshape(-1, channel_width)
    lookup_vectors = (
        jnp.dot(all_flat, lookup_weights, preferred_element_type=jnp.float32)
        .astype(jnp.bfloat16)
        .reshape(row_total, key_count, channel_width)
    )
    content_vectors = (
        jnp.dot(all_flat, content_weights, preferred_element_type=jnp.float32)
        .astype(jnp.bfloat16)
        .reshape(row_total, key_count, channel_width)
    )
    dbias_init = jnp.zeros(bias_full.shape, jnp.float32)
    dbias_local, row_results = lax.scan(
        functools.partial(row_backward, bias_full, head_count),
        dbias_init,
        (probe_vectors, lookup_vectors, content_vectors, sigmoid_factors, derivative_modulated),
    )
    (
        modulated_result,
        derivative_logits_sigmoid,
        derivative_probe_weights,
        derivative_lookup_weights,
        derivative_content_weights,
    ) = row_results
    key_weight_wide = lookup_weights.astype(jnp.float32)
    value_weight_wide = content_weights.astype(jnp.float32)
    lookup_plain = derivative_lookup_weights.reshape(-1, channel_width)
    content_plain = derivative_content_weights.reshape(-1, channel_width)
    key_term = (
        jnp.dot(lookup_plain, key_weight_wide.T, precision=highest)
        + jnp.dot(content_plain, value_weight_wide.T, precision=highest)
    ).reshape(row_total, -1, channel_width)
    grad_from_keys = lax.psum_scatter(key_term, "res", scatter_dimension=1, tiled=True).reshape(
        -1, channel_width
    )
    all_wide = all_flat.astype(jnp.float32)
    part_key = jnp.dot(all_wide.T, lookup_plain, precision=highest)
    part_value = jnp.dot(all_wide.T, content_plain, precision=highest)
    probe_plain = derivative_probe_weights.reshape(-1, channel_width)
    sigmoid_factor_plain = derivative_logits_sigmoid.reshape(-1, channel_width)
    part_query = jnp.dot(rescaled_plain.T, probe_plain, preferred_element_type=jnp.float32)
    part_gate = jnp.dot(rescaled_plain.T, sigmoid_factor_plain, preferred_element_type=jnp.float32)
    part_out = jnp.dot(
        modulated_result.reshape(-1, channel_width).T,
        incoming_slope_plain,
        preferred_element_type=jnp.float32,
    )
    derivative_rescaled = (
        jnp.dot(probe_plain, probe_weights.T, preferred_element_type=jnp.float32)
        + jnp.dot(sigmoid_factor_plain, sigmoid_weights.T, preferred_element_type=jnp.float32)
        + grad_from_keys
    )
    derivative_rescaled = derivative_rescaled.reshape(row_total, query_total, channel_width)
    part_gain = jnp.sum(derivative_rescaled * standardized_rows, axis=(0, 1))
    centered_scaled_gradient = derivative_rescaled * rescale_factor
    alignment_rows_gradient = (
        inverse_deviation
        * (
            centered_scaled_gradient
            - jnp.mean(centered_scaled_gradient, axis=-1, keepdims=True)
            - standardized_rows
            * jnp.mean(centered_scaled_gradient * standardized_rows, axis=-1, keepdims=True)
        )
    ).astype(jnp.bfloat16)
    dbias_own = lax.psum_scatter(dbias_local, "seq", scatter_dimension=2, tiled=True).astype(
        jnp.bfloat16
    )
    pair_input_gradient = jnp.einsum(
        "hij,ch->ijc", dbias_own, pair_bias_matrix, preferred_element_type=jnp.float32
    ).astype(jnp.bfloat16)
    part_bias = jnp.einsum(
        "ijc,hij->ch", pair_input_rows, dbias_own, preferred_element_type=jnp.float32
    )
    totals = lax.psum(
        (part_gain, part_query, part_key, part_value, part_gate, part_out, part_bias),
        ("seq", "res"),
    )
    return (
        alignment_rows_gradient,
        pair_input_gradient,
        totals[0],
        totals[1],
        totals[2],
        totals[3],
        totals[4],
        totals[5],
        totals[6],
    )


def solution(mesh):
    in_specs = (
        P("seq", "res", None),
        P("res", "seq", None),
        P("seq", "res", None),
        P(),
        P(),
        P(),
        P(),
        P(),
        P(),
        P(),
    )
    out_specs = (P("seq", "res", None), P("res", "seq", None), P(), P(), P(), P(), P(), P(), P())
    n_res, n_seq = mesh.shape["res"], mesh.shape["seq"]

    def run(*args):
        if n_res == args[-1].shape[1] and n_res & (n_res - 1) == 0 and n_seq > 1 and n_seq & (n_seq - 1) == 0:
            return by_head(n_res, n_seq, *args)
        return body(*args)

    return jax.shard_map(run, mesh=mesh, in_specs=in_specs, out_specs=out_specs, check_vma=False)
```

```python
import functools
import math

import jax
import jax.numpy as jnp
from jax import lax
from jax.experimental import pallas as pl
from jax.experimental.pallas import tpu as pltpu
from jax.sharding import PartitionSpec as P

F32 = jnp.float32
BF16 = jnp.bfloat16


def exchange(value, axis, size, offset):
    return lax.ppermute(value, axis, [(i, i ^ offset) for i in range(size)])


def dot(a, b, dims=((1,), (0,))):
    return lax.dot_general(a, b, (dims, ((), ())), preferred_element_type=F32)


def norm_rows(block):
    wide = block.astype(F32)
    centered = wide - jnp.mean(wide, axis=-1, keepdims=True)
    inverse = lax.rsqrt(jnp.mean(centered * centered, axis=-1, keepdims=True) + 1e-05)
    return centered * inverse, inverse


def place(r, k, own):
    return pl.ds(pl.multiple_of(jnp.bitwise_xor(r, k) * own, own), own)


def ready_kernel(own_ref, slope_ref, bias_ref, gate_w, out_w, gain_w, out_ref):
    heads, bias_rows, lanes = bias_ref.shape
    channels = gain_w.shape[1]
    width = channels // heads
    hat, _ = norm_rows(own_ref[...].reshape(-1, channels))
    normed = (hat * gain_w[...]).astype(BF16)
    gate = jax.nn.sigmoid(dot(normed, gate_w[...]))
    dgated = dot(slope_ref[...].reshape(-1, channels), out_w[...], ((1,), (1,)))
    datt = jnp.transpose((dgated * gate).astype(BF16).astype(F32)).astype(BF16)
    out_ref[:, :bias_rows, :] = bias_ref[...]
    for h in range(heads):
        for n in range(datt.shape[1] // lanes):
            at = bias_rows + n * width
            out_ref[h, at : at + width, :] = datt[h * width : (h + 1) * width, n * lanes : (n + 1) * lanes]


def pack(values, depth, own, out_ref):
    group = out_ref.shape[2] // own
    for b in range(out_ref.shape[0]):
        for n in range(values.shape[0] // group):
            block = [values[n * group + m, :depth, b * own : (b + 1) * own] for m in range(group)]
            out_ref[b, n * depth : (n + 1) * depth, :] = jnp.concatenate(block, axis=1).astype(BF16)


def attention_kernel(n_res, n_seq, width, span, where, *refs):
    tokens = refs[:2]
    biases, datts, head_w, gain_w, flow_ref, packed_ref, keep_ref, send_ref = refs[2:10]
    normed_s, datt_s, bias_s, dbias_s = refs[-4:]
    _, msa_rows, own, _ = tokens[0].shape
    r, s = where[0], where[1]
    total = own * n_res
    part = total // n_seq
    scale = 1.0 / math.sqrt(width)

    for m in range(n_seq):
        bias_s[:, m * part : (m + 1) * part] = biases[m]
    for k in range(n_res):
        for n in range(datts.shape[1] // width):
            block = jnp.transpose(datts[k, n * width : (n + 1) * width, :].astype(F32)).astype(BF16)
            for m in range(block.shape[0] // own):
                at = n * (block.shape[0] // own) + m
                datt_s[at, k * own : (k + 1) * own, :] = block[m * own : (m + 1) * own]
    dbias_s[...] = jnp.zeros_like(dbias_s)

    @pl.loop(0, msa_rows)
    def _(row):
        for k in range(n_res):
            hat, _ = norm_rows(tokens[k % 2][k // 2, row])
            normed_s[place(r & 1, k, own), :] = (hat * gain_w[...]).astype(BF16)

        normed = normed_s[...]
        weights = head_w[r]
        wq, wk, wv = (weights[n * width : (n + 1) * width] for n in range(3))
        rows = ((1,), (1,))
        q = dot(normed, wq, rows).astype(BF16)
        k_ = dot(normed, wk, rows).astype(BF16)
        v = dot(normed, wv, rows).astype(BF16)
        datt = datt_s[row]
        q_t, k_t, v_t, datt_t = (jnp.transpose(x) for x in (q, k_, v, datt))

        gk_t = jnp.zeros((width, total), F32)
        gv_t = jnp.zeros((width, total), F32)
        gqs, atts = [], []
        for c in range(total // span):
            lo, hi = c * span, (c + 1) * span
            scores = dot(q[lo:hi], k_t) * scale + bias_s[lo:hi, :].astype(F32)
            top = jnp.max(scores, axis=-1, keepdims=True)
            e = jnp.exp(scores - top)
            soft = e * (1.0 / jnp.sum(e, axis=-1, keepdims=True))
            half = soft.astype(BF16)
            atts.append(dot(half, v))
            gv_t += dot(datt_t[:, lo:hi], half)
            dsoft = dot(datt[lo:hi], v_t)
            inner = jnp.sum(soft * dsoft, axis=-1, keepdims=True)
            dscores = soft * (dsoft - inner)
            dbias_s[lo:hi, :] += dscores
            dhalf = dscores.astype(BF16)
            gqs.append(dot(dhalf, k_) * scale)
            gk_t += dot(q_t[:, lo:hi], dhalf)
        flow_ref[row, :width, :] = jnp.transpose(jnp.concatenate(gqs, axis=0))
        flow_ref[row, width : 2 * width, :] = gk_t * scale
        flow_ref[row, 2 * width : 3 * width, :] = gv_t
        flow_ref[row, 3 * width :, :] = jnp.transpose(jnp.concatenate(atts, axis=0))

    for m in range(n_seq):
        lane = pl.multiple_of(jnp.bitwise_xor(s, m) * part, part)
        at = m // 2 * total
        (send_ref if m % 2 else keep_ref)[at : at + total, :] = dbias_s[:, pl.ds(lane, part)]
    pack(flow_ref, 3 * width, own, packed_ref)


def gradient_kernel(n_res, width, where, *refs):
    tokens, slopes = refs[:2], refs[2 : 2 + n_res // 2]
    refs = refs[2 + n_res // 2 :]
    flow_ref, head_w, out_w, gain_w, grad_ref, keep_ref, send_ref = refs[:7]
    hat_s, normed_s, slope_s, gate_s, sums_s = refs[-5:]
    _, msa_rows, own, channels = tokens[0].shape
    r, s = where[0], where[1]

    sums_s[...] = jnp.zeros_like(sums_s)

    @pl.loop(0, msa_rows)
    def _(row):
        for k in range(n_res):
            hat, _ = norm_rows(tokens[k % 2][k // 2, row])
            hat_s[place(r & 1, k, own), :] = hat
            normed_s[place(r & 1, k, own), :] = (hat * gain_w[...]).astype(BF16)
            slope_s[place(r, k, own), :] = slopes[k // 2][k % 2, row]
        normed = normed_s[...]
        slope = slope_s[...]
        weights = head_w[r]
        rows = ((1,), (1,))
        gate = jax.nn.sigmoid(dot(weights[3 * width :], normed, rows))
        dgated = dot(out_w[r], slope, rows)
        att = flow_ref[row, 3 * width :, :]
        gated = (gate * att).astype(BF16)
        dgate = dgated * att * gate * (1.0 - gate)
        grad_t = jnp.concatenate([flow_ref[row, : 3 * width, :], dgate], axis=0)
        high_t = grad_t.astype(BF16)
        at = lax.broadcasted_iota(jnp.int32, grad_t.shape, 0)
        wide = (at >= width) & (at < 3 * width)
        low_t = jnp.where(wide, grad_t - high_t.astype(F32), 0.0).astype(BF16)
        high = jnp.transpose(grad_t).astype(BF16)
        low = jnp.transpose(low_t.astype(F32)).astype(BF16)
        sums_s[: 4 * width, :] += dot(high_t, normed) + dot(low_t, normed)
        sums_s[4 * width : 5 * width, :] += dot(gated, slope)
        grad_normed = dot(high, weights) + dot(low, weights)
        sums_s[5 * width : 5 * width + 1, :] += jnp.sum(grad_normed * hat_s[...], axis=0, keepdims=True)
        gate_s[row] = dgate

    side = channels // 2
    core = jnp.bitwise_and(s, 1)
    keep_ref[...] = sums_s[:, pl.ds(pl.multiple_of(core * side, side), side)]
    send_ref[...] = sums_s[:, pl.ds(pl.multiple_of((1 - core) * side, side), side)]
    pack(gate_s, width, own, grad_ref)


def weights_kernel(width, *refs):
    out = refs[-1]
    for n, ref in enumerate(refs[:-1]):
        flipped = jnp.transpose(ref[...].astype(F32)).astype(BF16)
        for h in range(out.shape[0]):
            out[h, n * width : (n + 1) * width, :] = flipped[h * width : (h + 1) * width]


def back_kernel(gain_at, pair_sum, pair_come, gates, keep, come, out_ref):
    n_res, first, _ = gates.shape
    own = pair_sum.shape[0] // n_res
    sums = keep[...] + come[...]
    half = sums.astype(BF16)
    rest = (sums - half.astype(F32))[gain_at:].astype(BF16)
    tail = jnp.concatenate([half[:gain_at], jnp.concatenate([half[gain_at:], rest], axis=0)], axis=0)
    for k in range(n_res):
        at = pl.ds(k * own, own)
        out_ref[k, :own, :] = (pair_sum[at, :] + pair_come[at, :]).astype(BF16)
        out_ref[k, own : own + first, :] = gates[k]
        out_ref[k, own + first :, :] = tail


def pair_kernel(grad_ref, rows_ref, out_ref, wide):
    wide[...] = grad_ref[:, : wide.shape[1], :].astype(F32)
    total = jnp.zeros(out_ref.shape[1:], F32)
    for i in range(rows_ref.shape[0]):
        total += dot(wide[:, i, :].astype(BF16), rows_ref[i])
    for n in range(out_ref.shape[0]):
        out_ref[n] = total


def tail_kernel(packed, back, own_ref, weights, gain_w, out_ref):
    heads, depth, channels = weights.shape
    width = depth // 4
    msa_rows, own, _ = own_ref.shape
    group = packed.shape[2] // own
    count = msa_rows // group
    first = own
    for n in range(count):
        total = jnp.zeros((group * own, channels), F32)
        for h in range(heads):
            block = [packed[h, n * 3 * width : (n + 1) * 3 * width], back[h, first + n * width : first + (n + 1) * width]]
            total += dot(jnp.concatenate(block, axis=0), weights[h], ((0,), (0,)))
        here = pl.ds(n * group, group)
        hat, inverse = norm_rows(own_ref[here].reshape(group * own, channels))
        g = total * gain_w[...]
        mean = jnp.mean(g, axis=-1, keepdims=True)
        cross = jnp.mean(g * hat, axis=-1, keepdims=True)
        out_ref[here] = (inverse * (g - mean - hat * cross)).astype(BF16).reshape(group, own, channels)


def sums_kernel(width, where, mine, other, gain_ref, *refs):
    outs, wide = refs[:-1], refs[-1]
    heads, _, side = mine.shape
    core = jnp.bitwise_and(where[1], 1)
    here = pl.ds(pl.multiple_of(core * side, side), side)
    there = pl.ds(pl.multiple_of((1 - core) * side, side), side)
    for ref, lanes in ((mine, here), (other, there)):
        extra = jnp.zeros((1, side), F32)
        for h in range(heads):
            block = ref[h, ref.shape[1] - 5 * width - 16 :, :].astype(F32)
            for n in range(5):
                wide[n, h * width : (h + 1) * width, lanes] = block[n * width : (n + 1) * width]
            extra += block[5 * width : 5 * width + 1] + block[5 * width + 8 : 5 * width + 9]
        gain_ref[:, lanes] = extra
    for n in range(4):
        outs[n][...] = jnp.transpose(wide[n])
    outs[4][...] = wide[4]


def whole(shape):
    return pl.BlockSpec(shape, lambda *_: (0,) * len(shape))


def by_head(
    n_res,
    n_seq,
    homolog_embedding,
    pair_input_rows,
    incoming_slope,
    rescale_factor,
    probe_weights,
    lookup_weights,
    content_weights,
    sigmoid_weights,
    final_projection,
    pair_bias_matrix,
):
    heads = pair_bias_matrix.shape[1]
    rows, own, channels = homolog_embedding.shape
    width = channels // heads
    total = own * n_res
    part = total // n_seq
    r, s = lax.axis_index("res"), lax.axis_index("seq")
    where = jnp.stack([r, s]).astype(jnp.int32)
    gain_row = rescale_factor.reshape(1, channels)

    def params(mib=48):
        return pltpu.CompilerParams(vmem_limit_bytes=mib * 1024 * 1024)

    bias_local = jnp.einsum(
        "ijc,ch->hij", pair_input_rows, pair_bias_matrix, preferred_element_type=F32
    ).astype(BF16)
    flat = rows * own // part * width
    ready = pl.pallas_call(
        ready_kernel,
        out_shape=jax.ShapeDtypeStruct((heads, own + flat, part), BF16),
        compiler_params=params(),
        name="ready",
    )(homolog_embedding, incoming_slope, bias_local, sigmoid_weights, final_projection, gain_row)
    ready = lax.all_to_all(ready, "res", 0, 0, tiled=True)
    lines = [list(range(n, n_res, 2)) for n in range(2)]
    tokens = lax.all_gather(homolog_embedding, "res", axis=0, axis_index_groups=lines)
    slope_pair = jnp.stack([incoming_slope, exchange(incoming_slope, "res", n_res, 1)])
    tokens, slope_pair = lax.optimization_barrier((tokens, slope_pair))
    tokens = [tokens, exchange(tokens, "res", n_res, 1)]
    datts = ready[:, own:]
    bias_all = lax.all_gather(ready[:, :own].reshape(total, part), "seq", axis=0)
    slopes = [slope_pair] + [exchange(slope_pair, "res", n_res, k) for k in range(2, n_res, 2)]

    head_weights = pl.pallas_call(
        functools.partial(weights_kernel, width),
        out_shape=jax.ShapeDtypeStruct((heads, 4 * width, channels), BF16),
        compiler_params=params(),
        name="weights",
    )(probe_weights, lookup_weights, content_weights, sigmoid_weights)
    out_weights = final_projection.reshape(heads, width, channels)

    token_spec = pl.BlockSpec((1, own, channels), lambda i, w: (i, 0, 0))
    flow_spec = pl.BlockSpec((1, 4 * width, total), lambda i, w: (i, 0, 0))
    weight_spec = pl.BlockSpec((1, 4 * width, channels), lambda i, w: (w[0], 0, 0))
    out_spec = pl.BlockSpec((1, width, channels), lambda i, w: (w[0], 0, 0))
    in_smem = pl.BlockSpec(memory_space=pltpu.SMEM)
    in_vmem = pl.BlockSpec(memory_space=pltpu.VMEM)
    sum_rows = 5 * width + 8
    side = channels // 2
    pair_rows = n_seq // 2 * total
    partial = jax.ShapeDtypeStruct((sum_rows, side), F32)
    flow, packed, pair_keep, pair_send = pl.pallas_call(
        functools.partial(attention_kernel, n_res, n_seq, width, total),
        in_specs=[in_smem] + [in_vmem] * 6,
        out_specs=[in_vmem] * 4,
        scratch_shapes=[
            pltpu.VMEM((total, channels), BF16),
            pltpu.VMEM((rows, total, width), BF16),
            pltpu.VMEM((total, total), BF16),
            pltpu.VMEM((total, total), F32),
        ],
        out_shape=[
            jax.ShapeDtypeStruct((rows, 4 * width, total), F32),
            jax.ShapeDtypeStruct((n_res, 3 * flat, part), BF16),
        ]
        + [jax.ShapeDtypeStruct((pair_rows, part), F32)] * 2,
        compiler_params=params(60),
        name="attention",
    )(where, *tokens, bias_all, datts, head_weights, gain_row)

    pair_send, *slopes = lax.optimization_barrier((pair_send, *slopes))
    keep, send, step = pair_keep, pair_send, 1
    while step < n_seq:
        pair_come = exchange(send, "seq", n_seq, step)
        step *= 2
        if step < n_seq:
            half = keep.shape[0] // 2
            send = keep[half:] + pair_come[half:]
            keep = keep[:half] + pair_come[:half]
            send, flow = lax.optimization_barrier((send, flow))
    pair_sum = keep

    grads, keep, send = pl.pallas_call(
        functools.partial(gradient_kernel, n_res, width),
        in_specs=[in_smem] + [in_vmem] * (n_res // 2 + 6),
        out_specs=[in_vmem] * 3,
        scratch_shapes=[
            pltpu.VMEM((total, channels), F32),
            pltpu.VMEM((total, channels), BF16),
            pltpu.VMEM((total, channels), BF16),
            pltpu.VMEM((rows, width, total), F32),
            pltpu.VMEM((sum_rows, channels), F32),
        ],
        out_shape=[jax.ShapeDtypeStruct((n_res, flat, part), BF16), partial, partial],
        compiler_params=params(60),
        name="gradients",
    )(where, *tokens, *slopes, flow, head_weights, out_weights, gain_row)

    packed = lax.all_to_all(packed, "res", 0, 0, tiled=True)
    pair_come, grads, send = lax.optimization_barrier((pair_come, grads, send))
    step = 1
    while step < n_seq:
        come = exchange(send, "seq", n_seq, step)
        step *= 2
        if step < n_seq:
            send, packed = lax.optimization_barrier((keep + come, packed))
            keep = send
    back_rows = own + flat + sum_rows + 8
    back = pl.pallas_call(
        functools.partial(back_kernel, 5 * width),
        out_shape=jax.ShapeDtypeStruct((n_res, back_rows, part), BF16),
        compiler_params=params(),
        name="back",
    )(pair_sum, pair_come, grads, keep, come)
    back = lax.all_to_all(back, "res", 0, 0, tiled=True)
    part_bias = pl.pallas_call(
        pair_kernel,
        out_shape=jax.ShapeDtypeStruct((n_seq * n_res, heads, pair_input_rows.shape[2]), F32),
        scratch_shapes=[pltpu.VMEM((n_res, own, part), F32)],
        compiler_params=params(),
        name="pair",
    )(back, pair_input_rows)

    part_bias, own_rows = lax.optimization_barrier((part_bias, homolog_embedding))
    other = exchange(back, "seq", n_seq, 1)
    part_bias = lax.all_to_all(part_bias, ("seq", "res"), 0, 0, tiled=True)
    pair_input_gradient = jnp.einsum(
        "hij,ch->ijc", back[:, :own], pair_bias_matrix, preferred_element_type=F32
    ).astype(BF16)

    alignment_rows_gradient = pl.pallas_call(
        tail_kernel,
        out_shape=jax.ShapeDtypeStruct(homolog_embedding.shape, BF16),
        compiler_params=params(),
        name="tail",
    )(packed, back, own_rows, head_weights, gain_row)

    square = jax.ShapeDtypeStruct((channels, channels), F32)
    gain, *weight_sums = pl.pallas_call(
        functools.partial(sums_kernel, width),
        grid_spec=pltpu.PrefetchScalarGridSpec(
            num_scalar_prefetch=1,
            grid=(1,),
            in_specs=[whole(back.shape)] * 2,
            out_specs=[whole((1, channels))] + [whole((channels, channels))] * 5,
            scratch_shapes=[pltpu.VMEM((5, channels, channels), F32)],
        ),
        out_shape=[jax.ShapeDtypeStruct((1, channels), F32)] + [square] * 5,
        compiler_params=params(),
        name="sums",
    )(where, back, other)
    part_bias, gain = lax.optimization_barrier((part_bias, gain))
    part_bias = part_bias.sum(axis=0)
    return (alignment_rows_gradient, pair_input_gradient, gain.reshape(channels), *weight_sums, part_bias.T)


def layer_norm_rows(alignment_block):
    content_vectors = alignment_block.astype(jnp.float32)
    centered = content_vectors - jnp.mean(content_vectors, axis=-1, keepdims=True)
    inverse_deviation = lax.rsqrt(jnp.mean(centered * centered, axis=-1, keepdims=True) + 1e-05)
    return (centered * inverse_deviation, inverse_deviation)


def row_backward(bias_full, head_count, dbias_total, row_inputs):
    probe_vectors, keys_row, values_row, gate_row, derivative_modulated = row_inputs
    query_total, channel_width = probe_vectors.shape
    key_count = keys_row.shape[0]
    head_width = channel_width // head_count
    softmax_scale = 1.0 / math.sqrt(head_width)
    query_heads = probe_vectors.reshape(query_total, head_count, head_width)
    key_heads = keys_row.reshape(key_count, head_count, head_width)
    value_heads = values_row.reshape(key_count, head_count, head_width)
    scores = (
        jnp.einsum("ihd,jhd->hij", query_heads, key_heads, preferred_element_type=jnp.float32)
        * softmax_scale
    )
    scores = scores + bias_full.astype(jnp.float32)
    weights_soft = jax.nn.softmax(scores, axis=-1)
    weights_half = weights_soft.astype(jnp.bfloat16)
    attended = jnp.einsum(
        "hij,jhd->ihd", weights_half, value_heads, preferred_element_type=jnp.float32
    ).reshape(query_total, channel_width)
    modulated_result = (gate_row * attended).astype(jnp.bfloat16)
    grad_attended = (derivative_modulated * gate_row).astype(jnp.bfloat16)
    derivative_logits_sigmoid = (
        derivative_modulated * attended * gate_row * (1.0 - gate_row)
    ).astype(jnp.bfloat16)
    grad_heads = grad_attended.reshape(query_total, head_count, head_width)
    grad_weights = jnp.einsum(
        "ihd,jhd->hij", grad_heads, value_heads, preferred_element_type=jnp.float32
    )
    row_inner = jnp.sum(weights_soft * grad_weights, axis=-1, keepdims=True)
    grad_scores = weights_soft * (grad_weights - row_inner)
    scores_half = grad_scores.astype(jnp.bfloat16)
    derivative_probe_weights = (
        jnp.einsum("hij,jhd->ihd", scores_half, key_heads, preferred_element_type=jnp.float32)
        * softmax_scale
    ).astype(jnp.bfloat16)
    derivative_lookup_weights = (
        jnp.einsum("hij,ihd->jhd", scores_half, query_heads, preferred_element_type=jnp.float32)
        * softmax_scale
    )
    derivative_content_weights = jnp.einsum(
        "hij,ihd->jhd", weights_half, grad_heads, preferred_element_type=jnp.float32
    )
    outputs = (
        modulated_result,
        derivative_logits_sigmoid,
        derivative_probe_weights.reshape(query_total, channel_width),
        derivative_lookup_weights.reshape(key_count, channel_width),
        derivative_content_weights.reshape(key_count, channel_width),
    )
    return (dbias_total + grad_scores, outputs)


def body(
    homolog_embedding,
    pair_input_rows,
    incoming_slope,
    rescale_factor,
    probe_weights,
    lookup_weights,
    content_weights,
    sigmoid_weights,
    final_projection,
    pair_bias_matrix,
):
    highest = lax.Precision.HIGHEST
    head_count = pair_bias_matrix.shape[1]
    row_total, query_total, channel_width = homolog_embedding.shape
    standardized_rows, inverse_deviation = layer_norm_rows(homolog_embedding)
    rescaled_embedding = (standardized_rows * rescale_factor).astype(jnp.bfloat16)
    rescaled_plain = rescaled_embedding.reshape(-1, channel_width)
    probe_vectors = (
        jnp.dot(rescaled_plain, probe_weights, preferred_element_type=jnp.float32)
        .astype(jnp.bfloat16)
        .reshape(row_total, query_total, channel_width)
    )
    sigmoid_factors = jax.nn.sigmoid(
        jnp.dot(rescaled_plain, sigmoid_weights, preferred_element_type=jnp.float32)
    ).reshape(row_total, query_total, channel_width)
    incoming_slope_plain = incoming_slope.reshape(-1, channel_width)
    derivative_modulated = jnp.dot(
        incoming_slope_plain, final_projection.T, preferred_element_type=jnp.float32
    ).reshape(row_total, query_total, channel_width)
    bias_local = jnp.einsum(
        "ijc,ch->hij", pair_input_rows, pair_bias_matrix, preferred_element_type=jnp.float32
    ).astype(jnp.bfloat16)
    bias_full = lax.all_gather(bias_local, "seq", axis=2, tiled=True)
    normed_all = lax.all_gather(rescaled_embedding, "res", axis=1, tiled=True)
    key_count = normed_all.shape[1]
    all_flat = normed_all.reshape(-1, channel_width)
    lookup_vectors = (
        jnp.dot(all_flat, lookup_weights, preferred_element_type=jnp.float32)
        .astype(jnp.bfloat16)
        .reshape(row_total, key_count, channel_width)
    )
    content_vectors = (
        jnp.dot(all_flat, content_weights, preferred_element_type=jnp.float32)
        .astype(jnp.bfloat16)
        .reshape(row_total, key_count, channel_width)
    )
    dbias_init = jnp.zeros(bias_full.shape, jnp.float32)
    dbias_local, row_results = lax.scan(
        functools.partial(row_backward, bias_full, head_count),
        dbias_init,
        (probe_vectors, lookup_vectors, content_vectors, sigmoid_factors, derivative_modulated),
    )
    (
        modulated_result,
        derivative_logits_sigmoid,
        derivative_probe_weights,
        derivative_lookup_weights,
        derivative_content_weights,
    ) = row_results
    key_weight_wide = lookup_weights.astype(jnp.float32)
    value_weight_wide = content_weights.astype(jnp.float32)
    lookup_plain = derivative_lookup_weights.reshape(-1, channel_width)
    content_plain = derivative_content_weights.reshape(-1, channel_width)
    key_term = (
        jnp.dot(lookup_plain, key_weight_wide.T, precision=highest)
        + jnp.dot(content_plain, value_weight_wide.T, precision=highest)
    ).reshape(row_total, -1, channel_width)
    grad_from_keys = lax.psum_scatter(key_term, "res", scatter_dimension=1, tiled=True).reshape(
        -1, channel_width
    )
    all_wide = all_flat.astype(jnp.float32)
    part_key = jnp.dot(all_wide.T, lookup_plain, precision=highest)
    part_value = jnp.dot(all_wide.T, content_plain, precision=highest)
    probe_plain = derivative_probe_weights.reshape(-1, channel_width)
    sigmoid_factor_plain = derivative_logits_sigmoid.reshape(-1, channel_width)
    part_query = jnp.dot(rescaled_plain.T, probe_plain, preferred_element_type=jnp.float32)
    part_gate = jnp.dot(rescaled_plain.T, sigmoid_factor_plain, preferred_element_type=jnp.float32)
    part_out = jnp.dot(
        modulated_result.reshape(-1, channel_width).T,
        incoming_slope_plain,
        preferred_element_type=jnp.float32,
    )
    derivative_rescaled = (
        jnp.dot(probe_plain, probe_weights.T, preferred_element_type=jnp.float32)
        + jnp.dot(sigmoid_factor_plain, sigmoid_weights.T, preferred_element_type=jnp.float32)
        + grad_from_keys
    )
    derivative_rescaled = derivative_rescaled.reshape(row_total, query_total, channel_width)
    part_gain = jnp.sum(derivative_rescaled * standardized_rows, axis=(0, 1))
    centered_scaled_gradient = derivative_rescaled * rescale_factor
    alignment_rows_gradient = (
        inverse_deviation
        * (
            centered_scaled_gradient
            - jnp.mean(centered_scaled_gradient, axis=-1, keepdims=True)
            - standardized_rows
            * jnp.mean(centered_scaled_gradient * standardized_rows, axis=-1, keepdims=True)
        )
    ).astype(jnp.bfloat16)
    dbias_own = lax.psum_scatter(dbias_local, "seq", scatter_dimension=2, tiled=True).astype(
        jnp.bfloat16
    )
    pair_input_gradient = jnp.einsum(
        "hij,ch->ijc", dbias_own, pair_bias_matrix, preferred_element_type=jnp.float32
    ).astype(jnp.bfloat16)
    part_bias = jnp.einsum(
        "ijc,hij->ch", pair_input_rows, dbias_own, preferred_element_type=jnp.float32
    )
    totals = lax.psum(
        (part_gain, part_query, part_key, part_value, part_gate, part_out, part_bias),
        ("seq", "res"),
    )
    return (
        alignment_rows_gradient,
        pair_input_gradient,
        totals[0],
        totals[1],
        totals[2],
        totals[3],
        totals[4],
        totals[5],
        totals[6],
    )


def solution(mesh):
    in_specs = (
        P("seq", "res", None),
        P("res", "seq", None),
        P("seq", "res", None),
        P(),
        P(),
        P(),
        P(),
        P(),
        P(),
        P(),
    )
    out_specs = (P("seq", "res", None), P("res", "seq", None), P(), P(), P(), P(), P(), P(), P())
    n_res, n_seq = mesh.shape["res"], mesh.shape["seq"]

    def run(*args):
        if n_res == args[-1].shape[1] and n_res & (n_res - 1) == 0 and n_seq > 1 and n_seq & (n_seq - 1) == 0:
            return by_head(n_res, n_seq, *args)
        return body(*args)

    return jax.shard_map(run, mesh=mesh, in_specs=in_specs, out_specs=out_specs, check_vma=False)
```

```python
import functools
import math

import jax
import jax.numpy as jnp
from jax import lax
from jax.experimental import pallas as pl
from jax.experimental.pallas import tpu as pltpu
from jax.sharding import PartitionSpec as P

F32 = jnp.float32
BF16 = jnp.bfloat16


def exchange(value, axis, size, offset):
    return lax.ppermute(value, axis, [(i, i ^ offset) for i in range(size)])


def dot(a, b, dims=((1,), (0,))):
    return lax.dot_general(a, b, (dims, ((), ())), preferred_element_type=F32)


def norm_rows(block):
    wide = block.astype(F32)
    centered = wide - jnp.mean(wide, axis=-1, keepdims=True)
    inverse = lax.rsqrt(jnp.mean(centered * centered, axis=-1, keepdims=True) + 1e-05)
    return centered * inverse, inverse


def place(r, k, own):
    return pl.ds(pl.multiple_of(jnp.bitwise_xor(r, k) * own, own), own)


def ready_kernel(own_ref, slope_ref, bias_ref, gate_w, out_w, gain_w, out_ref):
    heads, bias_rows, lanes = bias_ref.shape
    channels = gain_w.shape[1]
    width = channels // heads
    hat, _ = norm_rows(own_ref[...].reshape(-1, channels))
    normed = (hat * gain_w[...]).astype(BF16)
    gate = jax.nn.sigmoid(dot(normed, gate_w[...]))
    dgated = dot(slope_ref[...].reshape(-1, channels), out_w[...], ((1,), (1,)))
    datt = jnp.transpose((dgated * gate).astype(BF16).astype(F32)).astype(BF16)
    out_ref[:, :bias_rows, :] = bias_ref[...]
    for h in range(heads):
        for n in range(datt.shape[1] // lanes):
            at = bias_rows + n * width
            out_ref[h, at : at + width, :] = datt[h * width : (h + 1) * width, n * lanes : (n + 1) * lanes]


def pack(values, depth, own, out_ref):
    group = out_ref.shape[2] // own
    for b in range(out_ref.shape[0]):
        for n in range(values.shape[0] // group):
            block = [values[n * group + m, :depth, b * own : (b + 1) * own] for m in range(group)]
            out_ref[b, n * depth : (n + 1) * depth, :] = jnp.concatenate(block, axis=1).astype(BF16)


def attention_kernel(n_res, n_seq, width, span, where, *refs):
    tokens = refs[:2]
    biases, datts, head_w, gain_w, flow_ref, packed_ref, keep_ref, send_ref = refs[2:10]
    normed_s, datt_s, bias_s, dbias_s = refs[-4:]
    _, msa_rows, own, _ = tokens[0].shape
    r, s = where[0], where[1]
    total = own * n_res
    part = total // n_seq
    scale = 1.0 / math.sqrt(width)

    for m in range(n_seq):
        bias_s[:, m * part : (m + 1) * part] = biases[m]
    for k in range(n_res):
        for n in range(datts.shape[1] // width):
            block = jnp.transpose(datts[k, n * width : (n + 1) * width, :].astype(F32)).astype(BF16)
            for m in range(block.shape[0] // own):
                at = n * (block.shape[0] // own) + m
                datt_s[at, k * own : (k + 1) * own, :] = block[m * own : (m + 1) * own]
    dbias_s[...] = jnp.zeros_like(dbias_s)

    @pl.loop(0, msa_rows)
    def _(row):
        for k in range(n_res):
            hat, _ = norm_rows(tokens[k % 2][k // 2, row])
            normed_s[place(r & 1, k, own), :] = (hat * gain_w[...]).astype(BF16)

        normed = normed_s[...]
        weights = head_w[r]
        wq, wk, wv = (weights[n * width : (n + 1) * width] for n in range(3))
        rows = ((1,), (1,))
        q = dot(normed, wq, rows).astype(BF16)
        k_ = dot(normed, wk, rows).astype(BF16)
        v = dot(normed, wv, rows).astype(BF16)
        datt = datt_s[row]
        q_t, k_t, v_t, datt_t = (jnp.transpose(x) for x in (q, k_, v, datt))

        gk_t = jnp.zeros((width, total), F32)
        gv_t = jnp.zeros((width, total), F32)
        gqs, atts = [], []
        for c in range(total // span):
            lo, hi = c * span, (c + 1) * span
            scores = dot(q[lo:hi], k_t) * scale + bias_s[lo:hi, :].astype(F32)
            top = jnp.max(scores, axis=-1, keepdims=True)
            e = jnp.exp(scores - top)
            soft = e * (1.0 / jnp.sum(e, axis=-1, keepdims=True))
            half = soft.astype(BF16)
            atts.append(dot(half, v))
            gv_t += dot(datt_t[:, lo:hi], half)
            dsoft = dot(datt[lo:hi], v_t)
            inner = jnp.sum(soft * dsoft, axis=-1, keepdims=True)
            dscores = soft * (dsoft - inner)
            dbias_s[lo:hi, :] += dscores
            dhalf = dscores.astype(BF16)
            gqs.append(dot(dhalf, k_) * scale)
            gk_t += dot(q_t[:, lo:hi], dhalf)
        flow_ref[row, :width, :] = jnp.transpose(jnp.concatenate(gqs, axis=0))
        flow_ref[row, width : 2 * width, :] = gk_t * scale
        flow_ref[row, 2 * width : 3 * width, :] = gv_t
        flow_ref[row, 3 * width :, :] = jnp.transpose(jnp.concatenate(atts, axis=0))

    for m in range(n_seq):
        lane = pl.multiple_of(jnp.bitwise_xor(s, m) * part, part)
        at = m // 2 * total
        (send_ref if m % 2 else keep_ref)[at : at + total, :] = dbias_s[:, pl.ds(lane, part)]
    pack(flow_ref, 3 * width, own, packed_ref)


def gradient_kernel(n_res, width, where, *refs):
    tokens, slopes = refs[:2], refs[2 : 2 + n_res // 2]
    refs = refs[2 + n_res // 2 :]
    flow_ref, head_w, out_w, gain_w, grad_ref, keep_ref, send_ref = refs[:7]
    hat_s, normed_s, slope_s, gate_s, sums_s = refs[-5:]
    _, msa_rows, own, channels = tokens[0].shape
    r, s = where[0], where[1]

    sums_s[...] = jnp.zeros_like(sums_s)

    @pl.loop(0, msa_rows)
    def _(row):
        for k in range(n_res):
            hat, _ = norm_rows(tokens[k % 2][k // 2, row])
            hat_s[place(r & 1, k, own), :] = hat
            normed_s[place(r & 1, k, own), :] = (hat * gain_w[...]).astype(BF16)
            slope_s[place(r, k, own), :] = slopes[k // 2][k % 2, row]
        normed = normed_s[...]
        slope = slope_s[...]
        weights = head_w[r]
        rows = ((1,), (1,))
        gate = jax.nn.sigmoid(dot(weights[3 * width :], normed, rows))
        dgated = dot(out_w[r], slope, rows)
        att = flow_ref[row, 3 * width :, :]
        gated = (gate * att).astype(BF16)
        dgate = dgated * att * gate * (1.0 - gate)
        grad_t = jnp.concatenate([flow_ref[row, : 3 * width, :], dgate], axis=0)
        high_t = grad_t.astype(BF16)
        at = lax.broadcasted_iota(jnp.int32, grad_t.shape, 0)
        wide = (at >= width) & (at < 3 * width)
        low_t = jnp.where(wide, grad_t - high_t.astype(F32), 0.0).astype(BF16)
        high = jnp.transpose(grad_t).astype(BF16)
        low = jnp.transpose(low_t.astype(F32)).astype(BF16)
        sums_s[: 4 * width, :] += dot(high_t, normed) + dot(low_t, normed)
        sums_s[4 * width : 5 * width, :] += dot(gated, slope)
        grad_normed = dot(high, weights) + dot(low, weights)
        sums_s[5 * width : 5 * width + 1, :] += jnp.sum(grad_normed * hat_s[...], axis=0, keepdims=True)
        gate_s[row] = dgate

    side = channels // 2
    core = jnp.bitwise_and(s, 1)
    keep_ref[...] = sums_s[:, pl.ds(pl.multiple_of(core * side, side), side)]
    send_ref[...] = sums_s[:, pl.ds(pl.multiple_of((1 - core) * side, side), side)]
    pack(gate_s, width, own, grad_ref)


def weights_kernel(width, *refs):
    out = refs[-1]
    for n, ref in enumerate(refs[:-1]):
        flipped = jnp.transpose(ref[...].astype(F32)).astype(BF16)
        for h in range(out.shape[0]):
            out[h, n * width : (n + 1) * width, :] = flipped[h * width : (h + 1) * width]


def back_kernel(gain_at, pair_sum, pair_come, gates, keep, come, out_ref):
    n_res, first, _ = gates.shape
    own = pair_sum.shape[0] // n_res
    sums = keep[...] + come[...]
    half = sums.astype(BF16)
    rest = (sums - half.astype(F32))[gain_at:].astype(BF16)
    tail = jnp.concatenate([half[:gain_at], jnp.concatenate([half[gain_at:], rest], axis=0)], axis=0)
    for k in range(n_res):
        at = pl.ds(k * own, own)
        out_ref[k, :own, :] = (pair_sum[at, :] + pair_come[at, :]).astype(BF16)
        out_ref[k, own : own + first, :] = gates[k]
        out_ref[k, own + first :, :] = tail


def pair_kernel(grad_ref, rows_ref, out_ref, wide):
    wide[...] = grad_ref[:, : wide.shape[1], :].astype(F32)
    total = jnp.zeros(out_ref.shape[1:], F32)
    for i in range(rows_ref.shape[0]):
        total += dot(wide[:, i, :].astype(BF16), rows_ref[i])
    for n in range(out_ref.shape[0]):
        out_ref[n] = total


def tail_kernel(packed, back, own_ref, weights, gain_w, out_ref):
    heads, depth, channels = weights.shape
    width = depth // 4
    msa_rows, own, _ = own_ref.shape
    group = packed.shape[2] // own
    count = msa_rows // group
    first = own
    for n in range(count):
        total = jnp.zeros((group * own, channels), F32)
        for h in range(heads):
            block = [packed[h, n * 3 * width : (n + 1) * 3 * width], back[h, first + n * width : first + (n + 1) * width]]
            total += dot(jnp.concatenate(block, axis=0), weights[h], ((0,), (0,)))
        here = pl.ds(n * group, group)
        hat, inverse = norm_rows(own_ref[here].reshape(group * own, channels))
        g = total * gain_w[...]
        mean = jnp.mean(g, axis=-1, keepdims=True)
        cross = jnp.mean(g * hat, axis=-1, keepdims=True)
        out_ref[here] = (inverse * (g - mean - hat * cross)).astype(BF16).reshape(group, own, channels)


def sums_kernel(width, where, mine, other, gain_ref, *refs):
    outs, wide = refs[:-1], refs[-1]
    heads, _, side = mine.shape
    core = jnp.bitwise_and(where[1], 1)
    here = pl.ds(pl.multiple_of(core * side, side), side)
    there = pl.ds(pl.multiple_of((1 - core) * side, side), side)
    for ref, lanes in ((mine, here), (other, there)):
        extra = jnp.zeros((1, side), F32)
        for h in range(heads):
            block = ref[h, ref.shape[1] - 5 * width - 16 :, :].astype(F32)
            for n in range(5):
                wide[n, h * width : (h + 1) * width, lanes] = block[n * width : (n + 1) * width]
            extra += block[5 * width : 5 * width + 1] + block[5 * width + 8 : 5 * width + 9]
        gain_ref[:, lanes] = extra
    for n in range(4):
        outs[n][...] = jnp.transpose(wide[n])
    outs[4][...] = wide[4]


def whole(shape):
    return pl.BlockSpec(shape, lambda *_: (0,) * len(shape))


def by_head(
    n_res,
    n_seq,
    homolog_embedding,
    pair_input_rows,
    incoming_slope,
    rescale_factor,
    probe_weights,
    lookup_weights,
    content_weights,
    sigmoid_weights,
    final_projection,
    pair_bias_matrix,
):
    heads = pair_bias_matrix.shape[1]
    rows, own, channels = homolog_embedding.shape
    width = channels // heads
    total = own * n_res
    part = total // n_seq
    r, s = lax.axis_index("res"), lax.axis_index("seq")
    where = jnp.stack([r, s]).astype(jnp.int32)
    gain_row = rescale_factor.reshape(1, channels)

    def params(mib=48):
        return pltpu.CompilerParams(vmem_limit_bytes=mib * 1024 * 1024)

    bias_local = jnp.einsum(
        "ijc,ch->hij", pair_input_rows, pair_bias_matrix, preferred_element_type=F32
    ).astype(BF16)
    flat = rows * own // part * width
    ready = pl.pallas_call(
        ready_kernel,
        out_shape=jax.ShapeDtypeStruct((heads, own + flat, part), BF16),
        compiler_params=params(),
        name="ready",
    )(homolog_embedding, incoming_slope, bias_local, sigmoid_weights, final_projection, gain_row)
    ready = lax.all_to_all(ready, "res", 0, 0, tiled=True)
    lines = [list(range(n, n_res, 2)) for n in range(2)]
    tokens = lax.all_gather(homolog_embedding, "res", axis=0, axis_index_groups=lines)
    slope_pair = jnp.stack([incoming_slope, exchange(incoming_slope, "res", n_res, 1)])
    tokens, slope_pair = lax.optimization_barrier((tokens, slope_pair))
    tokens = [tokens, exchange(tokens, "res", n_res, 1)]
    datts = ready[:, own:]
    bias_all = lax.all_gather(ready[:, :own].reshape(total, part), "seq", axis=0)
    slopes = [slope_pair] + [exchange(slope_pair, "res", n_res, k) for k in range(2, n_res, 2)]

    head_weights = pl.pallas_call(
        functools.partial(weights_kernel, width),
        out_shape=jax.ShapeDtypeStruct((heads, 4 * width, channels), BF16),
        compiler_params=params(),
        name="weights",
    )(probe_weights, lookup_weights, content_weights, sigmoid_weights)
    out_weights = final_projection.reshape(heads, width, channels)

    token_spec = pl.BlockSpec((1, own, channels), lambda i, w: (i, 0, 0))
    flow_spec = pl.BlockSpec((1, 4 * width, total), lambda i, w: (i, 0, 0))
    weight_spec = pl.BlockSpec((1, 4 * width, channels), lambda i, w: (w[0], 0, 0))
    out_spec = pl.BlockSpec((1, width, channels), lambda i, w: (w[0], 0, 0))
    in_smem = pl.BlockSpec(memory_space=pltpu.SMEM)
    in_vmem = pl.BlockSpec(memory_space=pltpu.VMEM)
    sum_rows = 5 * width + 8
    side = channels // 2
    pair_rows = n_seq // 2 * total
    partial = jax.ShapeDtypeStruct((sum_rows, side), F32)
    flow, packed, pair_keep, pair_send = pl.pallas_call(
        functools.partial(attention_kernel, n_res, n_seq, width, total),
        in_specs=[in_smem] + [in_vmem] * 6,
        out_specs=[in_vmem] * 4,
        scratch_shapes=[
            pltpu.VMEM((total, channels), BF16),
            pltpu.VMEM((rows, total, width), BF16),
            pltpu.VMEM((total, total), BF16),
            pltpu.VMEM((total, total), F32),
        ],
        out_shape=[
            jax.ShapeDtypeStruct((rows, 4 * width, total), F32),
            jax.ShapeDtypeStruct((n_res, 3 * flat, part), BF16),
        ]
        + [jax.ShapeDtypeStruct((pair_rows, part), F32)] * 2,
        compiler_params=params(32),
        name="attention",
    )(where, *tokens, bias_all, datts, head_weights, gain_row)

    pair_send, *slopes = lax.optimization_barrier((pair_send, *slopes))
    keep, send, step = pair_keep, pair_send, 1
    while step < n_seq:
        pair_come = exchange(send, "seq", n_seq, step)
        step *= 2
        if step < n_seq:
            half = keep.shape[0] // 2
            send = keep[half:] + pair_come[half:]
            keep = keep[:half] + pair_come[:half]
            send, flow = lax.optimization_barrier((send, flow))
    pair_sum = keep

    grads, keep, send = pl.pallas_call(
        functools.partial(gradient_kernel, n_res, width),
        in_specs=[in_smem] + [in_vmem] * (n_res // 2 + 6),
        out_specs=[in_vmem] * 3,
        scratch_shapes=[
            pltpu.VMEM((total, channels), F32),
            pltpu.VMEM((total, channels), BF16),
            pltpu.VMEM((total, channels), BF16),
            pltpu.VMEM((rows, width, total), F32),
            pltpu.VMEM((sum_rows, channels), F32),
        ],
        out_shape=[jax.ShapeDtypeStruct((n_res, flat, part), BF16), partial, partial],
        compiler_params=params(32),
        name="gradients",
    )(where, *tokens, *slopes, flow, head_weights, out_weights, gain_row)

    packed = lax.all_to_all(packed, "res", 0, 0, tiled=True)
    step = 1
    while step < n_seq:
        come = exchange(send, "seq", n_seq, step)
        step *= 2
        if step < n_seq:
            send, pair_come = lax.optimization_barrier((keep + come, pair_come))
            keep = send
    come, packed = lax.optimization_barrier((come, packed))
    back_rows = own + flat + sum_rows + 8
    back = pl.pallas_call(
        functools.partial(back_kernel, 5 * width),
        out_shape=jax.ShapeDtypeStruct((n_res, back_rows, part), BF16),
        compiler_params=params(),
        name="back",
    )(pair_sum, pair_come, grads, keep, come)
    back = lax.all_to_all(back, "res", 0, 0, tiled=True)
    part_bias = pl.pallas_call(
        pair_kernel,
        out_shape=jax.ShapeDtypeStruct((n_seq * n_res, heads, pair_input_rows.shape[2]), F32),
        scratch_shapes=[pltpu.VMEM((n_res, own, part), F32)],
        compiler_params=params(),
        name="pair",
    )(back, pair_input_rows)

    part_bias, own_rows = lax.optimization_barrier((part_bias, homolog_embedding))
    other = exchange(back, "seq", n_seq, 1)
    part_bias = lax.all_to_all(part_bias, ("seq", "res"), 0, 0, tiled=True)
    pair_input_gradient = jnp.einsum(
        "hij,ch->ijc", back[:, :own], pair_bias_matrix, preferred_element_type=F32
    ).astype(BF16)

    alignment_rows_gradient = pl.pallas_call(
        tail_kernel,
        out_shape=jax.ShapeDtypeStruct(homolog_embedding.shape, BF16),
        compiler_params=params(),
        name="tail",
    )(packed, back, own_rows, head_weights, gain_row)

    square = jax.ShapeDtypeStruct((channels, channels), F32)
    gain, *weight_sums = pl.pallas_call(
        functools.partial(sums_kernel, width),
        grid_spec=pltpu.PrefetchScalarGridSpec(
            num_scalar_prefetch=1,
            grid=(1,),
            in_specs=[whole(back.shape)] * 2,
            out_specs=[whole((1, channels))] + [whole((channels, channels))] * 5,
            scratch_shapes=[pltpu.VMEM((5, channels, channels), F32)],
        ),
        out_shape=[jax.ShapeDtypeStruct((1, channels), F32)] + [square] * 5,
        compiler_params=params(),
        name="sums",
    )(where, back, other)
    part_bias, gain = lax.optimization_barrier((part_bias, gain))
    part_bias = part_bias.sum(axis=0)
    return (alignment_rows_gradient, pair_input_gradient, gain.reshape(channels), *weight_sums, part_bias.T)


def layer_norm_rows(alignment_block):
    content_vectors = alignment_block.astype(jnp.float32)
    centered = content_vectors - jnp.mean(content_vectors, axis=-1, keepdims=True)
    inverse_deviation = lax.rsqrt(jnp.mean(centered * centered, axis=-1, keepdims=True) + 1e-05)
    return (centered * inverse_deviation, inverse_deviation)


def row_backward(bias_full, head_count, dbias_total, row_inputs):
    probe_vectors, keys_row, values_row, gate_row, derivative_modulated = row_inputs
    query_total, channel_width = probe_vectors.shape
    key_count = keys_row.shape[0]
    head_width = channel_width // head_count
    softmax_scale = 1.0 / math.sqrt(head_width)
    query_heads = probe_vectors.reshape(query_total, head_count, head_width)
    key_heads = keys_row.reshape(key_count, head_count, head_width)
    value_heads = values_row.reshape(key_count, head_count, head_width)
    scores = (
        jnp.einsum("ihd,jhd->hij", query_heads, key_heads, preferred_element_type=jnp.float32)
        * softmax_scale
    )
    scores = scores + bias_full.astype(jnp.float32)
    weights_soft = jax.nn.softmax(scores, axis=-1)
    weights_half = weights_soft.astype(jnp.bfloat16)
    attended = jnp.einsum(
        "hij,jhd->ihd", weights_half, value_heads, preferred_element_type=jnp.float32
    ).reshape(query_total, channel_width)
    modulated_result = (gate_row * attended).astype(jnp.bfloat16)
    grad_attended = (derivative_modulated * gate_row).astype(jnp.bfloat16)
    derivative_logits_sigmoid = (
        derivative_modulated * attended * gate_row * (1.0 - gate_row)
    ).astype(jnp.bfloat16)
    grad_heads = grad_attended.reshape(query_total, head_count, head_width)
    grad_weights = jnp.einsum(
        "ihd,jhd->hij", grad_heads, value_heads, preferred_element_type=jnp.float32
    )
    row_inner = jnp.sum(weights_soft * grad_weights, axis=-1, keepdims=True)
    grad_scores = weights_soft * (grad_weights - row_inner)
    scores_half = grad_scores.astype(jnp.bfloat16)
    derivative_probe_weights = (
        jnp.einsum("hij,jhd->ihd", scores_half, key_heads, preferred_element_type=jnp.float32)
        * softmax_scale
    ).astype(jnp.bfloat16)
    derivative_lookup_weights = (
        jnp.einsum("hij,ihd->jhd", scores_half, query_heads, preferred_element_type=jnp.float32)
        * softmax_scale
    )
    derivative_content_weights = jnp.einsum(
        "hij,ihd->jhd", weights_half, grad_heads, preferred_element_type=jnp.float32
    )
    outputs = (
        modulated_result,
        derivative_logits_sigmoid,
        derivative_probe_weights.reshape(query_total, channel_width),
        derivative_lookup_weights.reshape(key_count, channel_width),
        derivative_content_weights.reshape(key_count, channel_width),
    )
    return (dbias_total + grad_scores, outputs)


def body(
    homolog_embedding,
    pair_input_rows,
    incoming_slope,
    rescale_factor,
    probe_weights,
    lookup_weights,
    content_weights,
    sigmoid_weights,
    final_projection,
    pair_bias_matrix,
):
    highest = lax.Precision.HIGHEST
    head_count = pair_bias_matrix.shape[1]
    row_total, query_total, channel_width = homolog_embedding.shape
    standardized_rows, inverse_deviation = layer_norm_rows(homolog_embedding)
    rescaled_embedding = (standardized_rows * rescale_factor).astype(jnp.bfloat16)
    rescaled_plain = rescaled_embedding.reshape(-1, channel_width)
    probe_vectors = (
        jnp.dot(rescaled_plain, probe_weights, preferred_element_type=jnp.float32)
        .astype(jnp.bfloat16)
        .reshape(row_total, query_total, channel_width)
    )
    sigmoid_factors = jax.nn.sigmoid(
        jnp.dot(rescaled_plain, sigmoid_weights, preferred_element_type=jnp.float32)
    ).reshape(row_total, query_total, channel_width)
    incoming_slope_plain = incoming_slope.reshape(-1, channel_width)
    derivative_modulated = jnp.dot(
        incoming_slope_plain, final_projection.T, preferred_element_type=jnp.float32
    ).reshape(row_total, query_total, channel_width)
    bias_local = jnp.einsum(
        "ijc,ch->hij", pair_input_rows, pair_bias_matrix, preferred_element_type=jnp.float32
    ).astype(jnp.bfloat16)
    bias_full = lax.all_gather(bias_local, "seq", axis=2, tiled=True)
    normed_all = lax.all_gather(rescaled_embedding, "res", axis=1, tiled=True)
    key_count = normed_all.shape[1]
    all_flat = normed_all.reshape(-1, channel_width)
    lookup_vectors = (
        jnp.dot(all_flat, lookup_weights, preferred_element_type=jnp.float32)
        .astype(jnp.bfloat16)
        .reshape(row_total, key_count, channel_width)
    )
    content_vectors = (
        jnp.dot(all_flat, content_weights, preferred_element_type=jnp.float32)
        .astype(jnp.bfloat16)
        .reshape(row_total, key_count, channel_width)
    )
    dbias_init = jnp.zeros(bias_full.shape, jnp.float32)
    dbias_local, row_results = lax.scan(
        functools.partial(row_backward, bias_full, head_count),
        dbias_init,
        (probe_vectors, lookup_vectors, content_vectors, sigmoid_factors, derivative_modulated),
    )
    (
        modulated_result,
        derivative_logits_sigmoid,
        derivative_probe_weights,
        derivative_lookup_weights,
        derivative_content_weights,
    ) = row_results
    key_weight_wide = lookup_weights.astype(jnp.float32)
    value_weight_wide = content_weights.astype(jnp.float32)
    lookup_plain = derivative_lookup_weights.reshape(-1, channel_width)
    content_plain = derivative_content_weights.reshape(-1, channel_width)
    key_term = (
        jnp.dot(lookup_plain, key_weight_wide.T, precision=highest)
        + jnp.dot(content_plain, value_weight_wide.T, precision=highest)
    ).reshape(row_total, -1, channel_width)
    grad_from_keys = lax.psum_scatter(key_term, "res", scatter_dimension=1, tiled=True).reshape(
        -1, channel_width
    )
    all_wide = all_flat.astype(jnp.float32)
    part_key = jnp.dot(all_wide.T, lookup_plain, precision=highest)
    part_value = jnp.dot(all_wide.T, content_plain, precision=highest)
    probe_plain = derivative_probe_weights.reshape(-1, channel_width)
    sigmoid_factor_plain = derivative_logits_sigmoid.reshape(-1, channel_width)
    part_query = jnp.dot(rescaled_plain.T, probe_plain, preferred_element_type=jnp.float32)
    part_gate = jnp.dot(rescaled_plain.T, sigmoid_factor_plain, preferred_element_type=jnp.float32)
    part_out = jnp.dot(
        modulated_result.reshape(-1, channel_width).T,
        incoming_slope_plain,
        preferred_element_type=jnp.float32,
    )
    derivative_rescaled = (
        jnp.dot(probe_plain, probe_weights.T, preferred_element_type=jnp.float32)
        + jnp.dot(sigmoid_factor_plain, sigmoid_weights.T, preferred_element_type=jnp.float32)
        + grad_from_keys
    )
    derivative_rescaled = derivative_rescaled.reshape(row_total, query_total, channel_width)
    part_gain = jnp.sum(derivative_rescaled * standardized_rows, axis=(0, 1))
    centered_scaled_gradient = derivative_rescaled * rescale_factor
    alignment_rows_gradient = (
        inverse_deviation
        * (
            centered_scaled_gradient
            - jnp.mean(centered_scaled_gradient, axis=-1, keepdims=True)
            - standardized_rows
            * jnp.mean(centered_scaled_gradient * standardized_rows, axis=-1, keepdims=True)
        )
    ).astype(jnp.bfloat16)
    dbias_own = lax.psum_scatter(dbias_local, "seq", scatter_dimension=2, tiled=True).astype(
        jnp.bfloat16
    )
    pair_input_gradient = jnp.einsum(
        "hij,ch->ijc", dbias_own, pair_bias_matrix, preferred_element_type=jnp.float32
    ).astype(jnp.bfloat16)
    part_bias = jnp.einsum(
        "ijc,hij->ch", pair_input_rows, dbias_own, preferred_element_type=jnp.float32
    )
    totals = lax.psum(
        (part_gain, part_query, part_key, part_value, part_gate, part_out, part_bias),
        ("seq", "res"),
    )
    return (
        alignment_rows_gradient,
        pair_input_gradient,
        totals[0],
        totals[1],
        totals[2],
        totals[3],
        totals[4],
        totals[5],
        totals[6],
    )


def solution(mesh):
    in_specs = (
        P("seq", "res", None),
        P("res", "seq", None),
        P("seq", "res", None),
        P(),
        P(),
        P(),
        P(),
        P(),
        P(),
        P(),
    )
    out_specs = (P("seq", "res", None), P("res", "seq", None), P(), P(), P(), P(), P(), P(), P())
    n_res, n_seq = mesh.shape["res"], mesh.shape["seq"]

    def run(*args):
        if n_res == args[-1].shape[1] and n_res & (n_res - 1) == 0 and n_seq > 1 and n_seq & (n_seq - 1) == 0:
            return by_head(n_res, n_seq, *args)
        return body(*args)

    return jax.shard_map(run, mesh=mesh, in_specs=in_specs, out_specs=out_specs, check_vma=False)
```

```python
import functools
import math

import jax
import jax.numpy as jnp
from jax import lax
from jax.experimental import pallas as pl
from jax.experimental.pallas import tpu as pltpu
from jax.sharding import PartitionSpec as P

F32 = jnp.float32
BF16 = jnp.bfloat16
LOG2E = 1.0 / math.log(2.0)


def exchange(value, axis, size, offset):
    return lax.ppermute(value, axis, [(i, i ^ offset) for i in range(size)])


def dot(a, b, dims=((1,), (0,))):
    return lax.dot_general(a, b, (dims, ((), ())), preferred_element_type=F32)


def norm_rows(block):
    wide = block.astype(F32)
    centered = wide - jnp.mean(wide, axis=-1, keepdims=True)
    inverse = lax.rsqrt(jnp.mean(centered * centered, axis=-1, keepdims=True) + 1e-05)
    return centered * inverse, inverse


def place(r, k, own):
    return pl.ds(pl.multiple_of(jnp.bitwise_xor(r, k) * own, own), own)


def ready_kernel(own_ref, slope_ref, bias_ref, gate_w, out_w, gain_w, out_ref):
    heads, bias_rows, lanes = bias_ref.shape
    channels = gain_w.shape[1]
    width = channels // heads
    hat, _ = norm_rows(own_ref[...].reshape(-1, channels))
    normed = (hat * gain_w[...]).astype(BF16)
    gate = jax.nn.sigmoid(dot(normed, gate_w[...]))
    dgated = dot(slope_ref[...].reshape(-1, channels), out_w[...], ((1,), (1,)))
    datt = jnp.transpose((dgated * gate).astype(BF16).astype(F32)).astype(BF16)
    out_ref[:, :bias_rows, :] = bias_ref[...]
    for h in range(heads):
        for n in range(datt.shape[1] // lanes):
            at = bias_rows + n * width
            out_ref[h, at : at + width, :] = datt[h * width : (h + 1) * width, n * lanes : (n + 1) * lanes]


def pack(values, depth, own, out_ref):
    group = out_ref.shape[2] // own
    for b in range(out_ref.shape[0]):
        for n in range(values.shape[0] // group):
            block = [values[n * group + m, :depth, b * own : (b + 1) * own] for m in range(group)]
            out_ref[b, n * depth : (n + 1) * depth, :] = jnp.concatenate(block, axis=1).astype(BF16)


def attention_kernel(n_res, n_seq, width, span, where, *refs):
    tokens = refs[:2]
    biases, datts, head_w, gain_w, flow_ref, packed_ref, keep_ref, send_ref = refs[2:10]
    normed_s, datt_s, bias_s, dbias_s = refs[-4:]
    _, msa_rows, own, _ = tokens[0].shape
    r, s = where[0], where[1]
    total = own * n_res
    part = total // n_seq
    scale = 1.0 / math.sqrt(width)

    for m in range(n_seq):
        bias_s[:, m * part : (m + 1) * part] = biases[m].astype(F32) * LOG2E
    for k in range(n_res):
        for n in range(datts.shape[1] // width):
            block = jnp.transpose(datts[k, n * width : (n + 1) * width, :].astype(F32)).astype(BF16)
            for m in range(block.shape[0] // own):
                at = n * (block.shape[0] // own) + m
                datt_s[at, k * own : (k + 1) * own, :] = block[m * own : (m + 1) * own]
    dbias_s[...] = jnp.zeros_like(dbias_s)

    @pl.loop(0, msa_rows)
    def _(row):
        for k in range(n_res):
            hat, _ = norm_rows(tokens[k % 2][k // 2, row])
            normed_s[place(r & 1, k, own), :] = (hat * gain_w[...]).astype(BF16)

        normed = normed_s[...]
        weights = head_w[r]
        wq, wk, wv = (weights[n * width : (n + 1) * width] for n in range(3))
        rows = ((1,), (1,))
        q = dot(normed, wq, rows).astype(BF16)
        k_ = dot(normed, wk, rows).astype(BF16)
        v = dot(normed, wv, rows).astype(BF16)
        datt = datt_s[row]
        q_t, k_t, v_t, datt_t = (jnp.transpose(x) for x in (q, k_, v, datt))

        gk_t = jnp.zeros((width, total), F32)
        gv_t = jnp.zeros((width, total), F32)
        gqs, atts = [], []
        for c in range(total // span):
            lo, hi = c * span, (c + 1) * span
            scores = dot(q[lo:hi], k_t) * (scale * LOG2E) + bias_s[lo:hi, :]
            top = jnp.max(scores, axis=-1, keepdims=True)
            e = jnp.exp2(scores - top)
            soft = e * (1.0 / jnp.sum(e, axis=-1, keepdims=True))
            half = soft.astype(BF16)
            atts.append(dot(half, v))
            gv_t += dot(datt_t[:, lo:hi], half)
            dsoft = dot(datt[lo:hi], v_t)
            inner = jnp.sum(soft * dsoft, axis=-1, keepdims=True)
            dscores = soft * (dsoft - inner)
            dbias_s[lo:hi, :] += dscores
            dhalf = dscores.astype(BF16)
            gqs.append(dot(dhalf, k_) * scale)
            gk_t += dot(q_t[:, lo:hi], dhalf)
        flow_ref[row, :width, :] = jnp.transpose(jnp.concatenate(gqs, axis=0))
        flow_ref[row, width : 2 * width, :] = gk_t * scale
        flow_ref[row, 2 * width : 3 * width, :] = gv_t
        flow_ref[row, 3 * width :, :] = jnp.transpose(jnp.concatenate(atts, axis=0))

    for m in range(n_seq):
        lane = pl.multiple_of(jnp.bitwise_xor(s, m) * part, part)
        at = m // 2 * total
        (send_ref if m % 2 else keep_ref)[at : at + total, :] = dbias_s[:, pl.ds(lane, part)]
    pack(flow_ref, 3 * width, own, packed_ref)


def gradient_kernel(n_res, width, where, *refs):
    tokens, slopes = refs[:2], refs[2 : 2 + n_res // 2]
    refs = refs[2 + n_res // 2 :]
    flow_ref, head_w, out_w, gain_w, grad_ref, keep_ref, send_ref = refs[:7]
    hat_s, normed_s, slope_s, gate_s, sums_s = refs[-5:]
    _, msa_rows, own, channels = tokens[0].shape
    r, s = where[0], where[1]

    sums_s[...] = jnp.zeros_like(sums_s)

    @pl.loop(0, msa_rows)
    def _(row):
        for k in range(n_res):
            hat, _ = norm_rows(tokens[k % 2][k // 2, row])
            hat_s[place(r & 1, k, own), :] = hat
            normed_s[place(r & 1, k, own), :] = (hat * gain_w[...]).astype(BF16)
            slope_s[place(r, k, own), :] = slopes[k // 2][k % 2, row]
        normed = normed_s[...]
        slope = slope_s[...]
        weights = head_w[r]
        rows = ((1,), (1,))
        gate = jax.nn.sigmoid(dot(weights[3 * width :], normed, rows))
        dgated = dot(out_w[r], slope, rows)
        att = flow_ref[row, 3 * width :, :]
        gated = (gate * att).astype(BF16)
        dgate = dgated * att * gate * (1.0 - gate)
        grad_t = jnp.concatenate([flow_ref[row, : 3 * width, :], dgate], axis=0)
        high_t = grad_t.astype(BF16)
        at = lax.broadcasted_iota(jnp.int32, grad_t.shape, 0)
        wide = (at >= width) & (at < 3 * width)
        low_t = jnp.where(wide, grad_t - high_t.astype(F32), 0.0).astype(BF16)
        high = jnp.transpose(grad_t).astype(BF16)
        low = jnp.transpose(low_t.astype(F32)).astype(BF16)
        sums_s[: 4 * width, :] += dot(high_t, normed) + dot(low_t, normed)
        sums_s[4 * width : 5 * width, :] += dot(gated, slope)
        grad_normed = dot(high, weights) + dot(low, weights)
        sums_s[5 * width : 5 * width + 1, :] += jnp.sum(grad_normed * hat_s[...], axis=0, keepdims=True)
        gate_s[row] = dgate

    side = channels // 2
    core = jnp.bitwise_and(s, 1)
    keep_ref[...] = sums_s[:, pl.ds(pl.multiple_of(core * side, side), side)]
    send_ref[...] = sums_s[:, pl.ds(pl.multiple_of((1 - core) * side, side), side)]
    pack(gate_s, width, own, grad_ref)


def weights_kernel(width, *refs):
    out = refs[-1]
    for n, ref in enumerate(refs[:-1]):
        flipped = jnp.transpose(ref[...].astype(F32)).astype(BF16)
        for h in range(out.shape[0]):
            out[h, n * width : (n + 1) * width, :] = flipped[h * width : (h + 1) * width]


def back_kernel(gain_at, pair_sum, pair_come, gates, keep, come, out_ref):
    n_res, first, _ = gates.shape
    own = pair_sum.shape[0] // n_res
    sums = keep[...] + come[...]
    half = sums.astype(BF16)
    rest = (sums - half.astype(F32))[gain_at:].astype(BF16)
    tail = jnp.concatenate([half[:gain_at], jnp.concatenate([half[gain_at:], rest], axis=0)], axis=0)
    for k in range(n_res):
        at = pl.ds(k * own, own)
        out_ref[k, :own, :] = (pair_sum[at, :] + pair_come[at, :]).astype(BF16)
        out_ref[k, own : own + first, :] = gates[k]
        out_ref[k, own + first :, :] = tail


def pair_kernel(grad_ref, rows_ref, out_ref, wide):
    wide[...] = grad_ref[:, : wide.shape[1], :].astype(F32)
    total = jnp.zeros(out_ref.shape[1:], F32)
    for i in range(rows_ref.shape[0]):
        total += dot(wide[:, i, :].astype(BF16), rows_ref[i])
    for n in range(out_ref.shape[0]):
        out_ref[n] = total


def tail_kernel(packed, back, own_ref, weights, gain_w, out_ref):
    heads, depth, channels = weights.shape
    width = depth // 4
    msa_rows, own, _ = own_ref.shape
    group = packed.shape[2] // own
    count = msa_rows // group
    first = own
    for n in range(count):
        total = jnp.zeros((group * own, channels), F32)
        for h in range(heads):
            block = [packed[h, n * 3 * width : (n + 1) * 3 * width], back[h, first + n * width : first + (n + 1) * width]]
            total += dot(jnp.concatenate(block, axis=0), weights[h], ((0,), (0,)))
        here = pl.ds(n * group, group)
        hat, inverse = norm_rows(own_ref[here].reshape(group * own, channels))
        g = total * gain_w[...]
        mean = jnp.mean(g, axis=-1, keepdims=True)
        cross = jnp.mean(g * hat, axis=-1, keepdims=True)
        out_ref[here] = (inverse * (g - mean - hat * cross)).astype(BF16).reshape(group, own, channels)


def sums_kernel(width, where, mine, other, gain_ref, *refs):
    outs, wide = refs[:-1], refs[-1]
    heads, _, side = mine.shape
    core = jnp.bitwise_and(where[1], 1)
    here = pl.ds(pl.multiple_of(core * side, side), side)
    there = pl.ds(pl.multiple_of((1 - core) * side, side), side)
    for ref, lanes in ((mine, here), (other, there)):
        extra = jnp.zeros((1, side), F32)
        for h in range(heads):
            block = ref[h, ref.shape[1] - 5 * width - 16 :, :].astype(F32)
            for n in range(5):
                wide[n, h * width : (h + 1) * width, lanes] = block[n * width : (n + 1) * width]
            extra += block[5 * width : 5 * width + 1] + block[5 * width + 8 : 5 * width + 9]
        gain_ref[:, lanes] = extra
    for n in range(4):
        outs[n][...] = jnp.transpose(wide[n])
    outs[4][...] = wide[4]


def whole(shape):
    return pl.BlockSpec(shape, lambda *_: (0,) * len(shape))


def by_head(
    n_res,
    n_seq,
    homolog_embedding,
    pair_input_rows,
    incoming_slope,
    rescale_factor,
    probe_weights,
    lookup_weights,
    content_weights,
    sigmoid_weights,
    final_projection,
    pair_bias_matrix,
):
    heads = pair_bias_matrix.shape[1]
    rows, own, channels = homolog_embedding.shape
    width = channels // heads
    total = own * n_res
    part = total // n_seq
    r, s = lax.axis_index("res"), lax.axis_index("seq")
    where = jnp.stack([r, s]).astype(jnp.int32)
    gain_row = rescale_factor.reshape(1, channels)

    def params(mib=48):
        return pltpu.CompilerParams(vmem_limit_bytes=mib * 1024 * 1024)

    bias_local = jnp.einsum(
        "ijc,ch->hij", pair_input_rows, pair_bias_matrix, preferred_element_type=F32
    ).astype(BF16)
    flat = rows * own // part * width
    ready = pl.pallas_call(
        ready_kernel,
        out_shape=jax.ShapeDtypeStruct((heads, own + flat, part), BF16),
        compiler_params=params(),
        name="ready",
    )(homolog_embedding, incoming_slope, bias_local, sigmoid_weights, final_projection, gain_row)
    ready = lax.all_to_all(ready, "res", 0, 0, tiled=True)
    lines = [list(range(n, n_res, 2)) for n in range(2)]
    tokens = lax.all_gather(homolog_embedding, "res", axis=0, axis_index_groups=lines)
    slope_pair = jnp.stack([incoming_slope, exchange(incoming_slope, "res", n_res, 1)])
    tokens, slope_pair = lax.optimization_barrier((tokens, slope_pair))
    tokens = [tokens, exchange(tokens, "res", n_res, 1)]
    datts = ready[:, own:]
    bias_all = lax.all_gather(ready[:, :own].reshape(total, part), "seq", axis=0)
    slopes = [slope_pair] + [exchange(slope_pair, "res", n_res, k) for k in range(2, n_res, 2)]

    head_weights = pl.pallas_call(
        functools.partial(weights_kernel, width),
        out_shape=jax.ShapeDtypeStruct((heads, 4 * width, channels), BF16),
        compiler_params=params(),
        name="weights",
    )(probe_weights, lookup_weights, content_weights, sigmoid_weights)
    out_weights = final_projection.reshape(heads, width, channels)

    token_spec = pl.BlockSpec((1, own, channels), lambda i, w: (i, 0, 0))
    flow_spec = pl.BlockSpec((1, 4 * width, total), lambda i, w: (i, 0, 0))
    weight_spec = pl.BlockSpec((1, 4 * width, channels), lambda i, w: (w[0], 0, 0))
    out_spec = pl.BlockSpec((1, width, channels), lambda i, w: (w[0], 0, 0))
    in_smem = pl.BlockSpec(memory_space=pltpu.SMEM)
    in_vmem = pl.BlockSpec(memory_space=pltpu.VMEM)
    sum_rows = 5 * width + 8
    side = channels // 2
    pair_rows = n_seq // 2 * total
    partial = jax.ShapeDtypeStruct((sum_rows, side), F32)
    flow, packed, pair_keep, pair_send = pl.pallas_call(
        functools.partial(attention_kernel, n_res, n_seq, width, total),
        in_specs=[in_smem] + [in_vmem] * 6,
        out_specs=[in_vmem] * 4,
        scratch_shapes=[
            pltpu.VMEM((total, channels), BF16),
            pltpu.VMEM((rows, total, width), BF16),
            pltpu.VMEM((total, total), F32),
            pltpu.VMEM((total, total), F32),
        ],
        out_shape=[
            jax.ShapeDtypeStruct((rows, 4 * width, total), F32),
            jax.ShapeDtypeStruct((n_res, 3 * flat, part), BF16),
        ]
        + [jax.ShapeDtypeStruct((pair_rows, part), F32)] * 2,
        compiler_params=params(32),
        name="attention",
    )(where, *tokens, bias_all, datts, head_weights, gain_row)

    pair_send, *slopes = lax.optimization_barrier((pair_send, *slopes))
    keep, send, step = pair_keep, pair_send, 1
    while step < n_seq:
        pair_come = exchange(send, "seq", n_seq, step)
        step *= 2
        if step < n_seq:
            half = keep.shape[0] // 2
            send = keep[half:] + pair_come[half:]
            keep = keep[:half] + pair_come[:half]
            send, flow = lax.optimization_barrier((send, flow))
    pair_sum = keep

    grads, keep, send = pl.pallas_call(
        functools.partial(gradient_kernel, n_res, width),
        in_specs=[in_smem] + [in_vmem] * (n_res // 2 + 6),
        out_specs=[in_vmem] * 3,
        scratch_shapes=[
            pltpu.VMEM((total, channels), F32),
            pltpu.VMEM((total, channels), BF16),
            pltpu.VMEM((total, channels), BF16),
            pltpu.VMEM((rows, width, total), F32),
            pltpu.VMEM((sum_rows, channels), F32),
        ],
        out_shape=[jax.ShapeDtypeStruct((n_res, flat, part), BF16), partial, partial],
        compiler_params=params(32),
        name="gradients",
    )(where, *tokens, *slopes, flow, head_weights, out_weights, gain_row)

    packed = lax.all_to_all(packed, "res", 0, 0, tiled=True)
    step = 1
    while step < n_seq:
        come = exchange(send, "seq", n_seq, step)
        step *= 2
        if step < n_seq:
            send, pair_come = lax.optimization_barrier((keep + come, pair_come))
            keep = send
    come, packed = lax.optimization_barrier((come, packed))
    back_rows = own + flat + sum_rows + 8
    back = pl.pallas_call(
        functools.partial(back_kernel, 5 * width),
        out_shape=jax.ShapeDtypeStruct((n_res, back_rows, part), BF16),
        compiler_params=params(),
        name="back",
    )(pair_sum, pair_come, grads, keep, come)
    back = lax.all_to_all(back, "res", 0, 0, tiled=True)
    part_bias = pl.pallas_call(
        pair_kernel,
        out_shape=jax.ShapeDtypeStruct((n_seq * n_res, heads, pair_input_rows.shape[2]), F32),
        scratch_shapes=[pltpu.VMEM((n_res, own, part), F32)],
        compiler_params=params(),
        name="pair",
    )(back, pair_input_rows)

    part_bias, own_rows = lax.optimization_barrier((part_bias, homolog_embedding))
    other = exchange(back, "seq", n_seq, 1)
    part_bias = lax.all_to_all(part_bias, ("seq", "res"), 0, 0, tiled=True)
    pair_input_gradient = jnp.einsum(
        "hij,ch->ijc", back[:, :own], pair_bias_matrix, preferred_element_type=F32
    ).astype(BF16)

    alignment_rows_gradient = pl.pallas_call(
        tail_kernel,
        out_shape=jax.ShapeDtypeStruct(homolog_embedding.shape, BF16),
        compiler_params=params(),
        name="tail",
    )(packed, back, own_rows, head_weights, gain_row)

    square = jax.ShapeDtypeStruct((channels, channels), F32)
    gain, *weight_sums = pl.pallas_call(
        functools.partial(sums_kernel, width),
        grid_spec=pltpu.PrefetchScalarGridSpec(
            num_scalar_prefetch=1,
            grid=(1,),
            in_specs=[whole(back.shape)] * 2,
            out_specs=[whole((1, channels))] + [whole((channels, channels))] * 5,
            scratch_shapes=[pltpu.VMEM((5, channels, channels), F32)],
        ),
        out_shape=[jax.ShapeDtypeStruct((1, channels), F32)] + [square] * 5,
        compiler_params=params(),
        name="sums",
    )(where, back, other)
    part_bias, gain = lax.optimization_barrier((part_bias, gain))
    part_bias = part_bias.sum(axis=0)
    return (alignment_rows_gradient, pair_input_gradient, gain.reshape(channels), *weight_sums, part_bias.T)


def layer_norm_rows(alignment_block):
    content_vectors = alignment_block.astype(jnp.float32)
    centered = content_vectors - jnp.mean(content_vectors, axis=-1, keepdims=True)
    inverse_deviation = lax.rsqrt(jnp.mean(centered * centered, axis=-1, keepdims=True) + 1e-05)
    return (centered * inverse_deviation, inverse_deviation)


def row_backward(bias_full, head_count, dbias_total, row_inputs):
    probe_vectors, keys_row, values_row, gate_row, derivative_modulated = row_inputs
    query_total, channel_width = probe_vectors.shape
    key_count = keys_row.shape[0]
    head_width = channel_width // head_count
    softmax_scale = 1.0 / math.sqrt(head_width)
    query_heads = probe_vectors.reshape(query_total, head_count, head_width)
    key_heads = keys_row.reshape(key_count, head_count, head_width)
    value_heads = values_row.reshape(key_count, head_count, head_width)
    scores = (
        jnp.einsum("ihd,jhd->hij", query_heads, key_heads, preferred_element_type=jnp.float32)
        * softmax_scale
    )
    scores = scores + bias_full.astype(jnp.float32)
    weights_soft = jax.nn.softmax(scores, axis=-1)
    weights_half = weights_soft.astype(jnp.bfloat16)
    attended = jnp.einsum(
        "hij,jhd->ihd", weights_half, value_heads, preferred_element_type=jnp.float32
    ).reshape(query_total, channel_width)
    modulated_result = (gate_row * attended).astype(jnp.bfloat16)
    grad_attended = (derivative_modulated * gate_row).astype(jnp.bfloat16)
    derivative_logits_sigmoid = (
        derivative_modulated * attended * gate_row * (1.0 - gate_row)
    ).astype(jnp.bfloat16)
    grad_heads = grad_attended.reshape(query_total, head_count, head_width)
    grad_weights = jnp.einsum(
        "ihd,jhd->hij", grad_heads, value_heads, preferred_element_type=jnp.float32
    )
    row_inner = jnp.sum(weights_soft * grad_weights, axis=-1, keepdims=True)
    grad_scores = weights_soft * (grad_weights - row_inner)
    scores_half = grad_scores.astype(jnp.bfloat16)
    derivative_probe_weights = (
        jnp.einsum("hij,jhd->ihd", scores_half, key_heads, preferred_element_type=jnp.float32)
        * softmax_scale
    ).astype(jnp.bfloat16)
    derivative_lookup_weights = (
        jnp.einsum("hij,ihd->jhd", scores_half, query_heads, preferred_element_type=jnp.float32)
        * softmax_scale
    )
    derivative_content_weights = jnp.einsum(
        "hij,ihd->jhd", weights_half, grad_heads, preferred_element_type=jnp.float32
    )
    outputs = (
        modulated_result,
        derivative_logits_sigmoid,
        derivative_probe_weights.reshape(query_total, channel_width),
        derivative_lookup_weights.reshape(key_count, channel_width),
        derivative_content_weights.reshape(key_count, channel_width),
    )
    return (dbias_total + grad_scores, outputs)


def body(
    homolog_embedding,
    pair_input_rows,
    incoming_slope,
    rescale_factor,
    probe_weights,
    lookup_weights,
    content_weights,
    sigmoid_weights,
    final_projection,
    pair_bias_matrix,
):
    highest = lax.Precision.HIGHEST
    head_count = pair_bias_matrix.shape[1]
    row_total, query_total, channel_width = homolog_embedding.shape
    standardized_rows, inverse_deviation = layer_norm_rows(homolog_embedding)
    rescaled_embedding = (standardized_rows * rescale_factor).astype(jnp.bfloat16)
    rescaled_plain = rescaled_embedding.reshape(-1, channel_width)
    probe_vectors = (
        jnp.dot(rescaled_plain, probe_weights, preferred_element_type=jnp.float32)
        .astype(jnp.bfloat16)
        .reshape(row_total, query_total, channel_width)
    )
    sigmoid_factors = jax.nn.sigmoid(
        jnp.dot(rescaled_plain, sigmoid_weights, preferred_element_type=jnp.float32)
    ).reshape(row_total, query_total, channel_width)
    incoming_slope_plain = incoming_slope.reshape(-1, channel_width)
    derivative_modulated = jnp.dot(
        incoming_slope_plain, final_projection.T, preferred_element_type=jnp.float32
    ).reshape(row_total, query_total, channel_width)
    bias_local = jnp.einsum(
        "ijc,ch->hij", pair_input_rows, pair_bias_matrix, preferred_element_type=jnp.float32
    ).astype(jnp.bfloat16)
    bias_full = lax.all_gather(bias_local, "seq", axis=2, tiled=True)
    normed_all = lax.all_gather(rescaled_embedding, "res", axis=1, tiled=True)
    key_count = normed_all.shape[1]
    all_flat = normed_all.reshape(-1, channel_width)
    lookup_vectors = (
        jnp.dot(all_flat, lookup_weights, preferred_element_type=jnp.float32)
        .astype(jnp.bfloat16)
        .reshape(row_total, key_count, channel_width)
    )
    content_vectors = (
        jnp.dot(all_flat, content_weights, preferred_element_type=jnp.float32)
        .astype(jnp.bfloat16)
        .reshape(row_total, key_count, channel_width)
    )
    dbias_init = jnp.zeros(bias_full.shape, jnp.float32)
    dbias_local, row_results = lax.scan(
        functools.partial(row_backward, bias_full, head_count),
        dbias_init,
        (probe_vectors, lookup_vectors, content_vectors, sigmoid_factors, derivative_modulated),
    )
    (
        modulated_result,
        derivative_logits_sigmoid,
        derivative_probe_weights,
        derivative_lookup_weights,
        derivative_content_weights,
    ) = row_results
    key_weight_wide = lookup_weights.astype(jnp.float32)
    value_weight_wide = content_weights.astype(jnp.float32)
    lookup_plain = derivative_lookup_weights.reshape(-1, channel_width)
    content_plain = derivative_content_weights.reshape(-1, channel_width)
    key_term = (
        jnp.dot(lookup_plain, key_weight_wide.T, precision=highest)
        + jnp.dot(content_plain, value_weight_wide.T, precision=highest)
    ).reshape(row_total, -1, channel_width)
    grad_from_keys = lax.psum_scatter(key_term, "res", scatter_dimension=1, tiled=True).reshape(
        -1, channel_width
    )
    all_wide = all_flat.astype(jnp.float32)
    part_key = jnp.dot(all_wide.T, lookup_plain, precision=highest)
    part_value = jnp.dot(all_wide.T, content_plain, precision=highest)
    probe_plain = derivative_probe_weights.reshape(-1, channel_width)
    sigmoid_factor_plain = derivative_logits_sigmoid.reshape(-1, channel_width)
    part_query = jnp.dot(rescaled_plain.T, probe_plain, preferred_element_type=jnp.float32)
    part_gate = jnp.dot(rescaled_plain.T, sigmoid_factor_plain, preferred_element_type=jnp.float32)
    part_out = jnp.dot(
        modulated_result.reshape(-1, channel_width).T,
        incoming_slope_plain,
        preferred_element_type=jnp.float32,
    )
    derivative_rescaled = (
        jnp.dot(probe_plain, probe_weights.T, preferred_element_type=jnp.float32)
        + jnp.dot(sigmoid_factor_plain, sigmoid_weights.T, preferred_element_type=jnp.float32)
        + grad_from_keys
    )
    derivative_rescaled = derivative_rescaled.reshape(row_total, query_total, channel_width)
    part_gain = jnp.sum(derivative_rescaled * standardized_rows, axis=(0, 1))
    centered_scaled_gradient = derivative_rescaled * rescale_factor
    alignment_rows_gradient = (
        inverse_deviation
        * (
            centered_scaled_gradient
            - jnp.mean(centered_scaled_gradient, axis=-1, keepdims=True)
            - standardized_rows
            * jnp.mean(centered_scaled_gradient * standardized_rows, axis=-1, keepdims=True)
        )
    ).astype(jnp.bfloat16)
    dbias_own = lax.psum_scatter(dbias_local, "seq", scatter_dimension=2, tiled=True).astype(
        jnp.bfloat16
    )
    pair_input_gradient = jnp.einsum(
        "hij,ch->ijc", dbias_own, pair_bias_matrix, preferred_element_type=jnp.float32
    ).astype(jnp.bfloat16)
    part_bias = jnp.einsum(
        "ijc,hij->ch", pair_input_rows, dbias_own, preferred_element_type=jnp.float32
    )
    totals = lax.psum(
        (part_gain, part_query, part_key, part_value, part_gate, part_out, part_bias),
        ("seq", "res"),
    )
    return (
        alignment_rows_gradient,
        pair_input_gradient,
        totals[0],
        totals[1],
        totals[2],
        totals[3],
        totals[4],
        totals[5],
        totals[6],
    )


def solution(mesh):
    in_specs = (
        P("seq", "res", None),
        P("res", "seq", None),
        P("seq", "res", None),
        P(),
        P(),
        P(),
        P(),
        P(),
        P(),
        P(),
    )
    out_specs = (P("seq", "res", None), P("res", "seq", None), P(), P(), P(), P(), P(), P(), P())
    n_res, n_seq = mesh.shape["res"], mesh.shape["seq"]

    def run(*args):
        if n_res == args[-1].shape[1] and n_res & (n_res - 1) == 0 and n_seq > 1 and n_seq & (n_seq - 1) == 0:
            return by_head(n_res, n_seq, *args)
        return body(*args)

    return jax.shard_map(run, mesh=mesh, in_specs=in_specs, out_specs=out_specs, check_vma=False)
```
